32 devices in a mesh: ctx: 16 (over z, y, x), head: 2 (over core).
Axes of the slice: x: 2, y: 2, z: 4, core: 2. Of those that a mesh axis runs over, the one named last changes fastest.
Arguments:
- softmax_query: bfloat16 [2048, 1024], P('ctx', 'head'), may hold values from -6 to 6
- softmax_key: bfloat16 [2048, 1024], P('ctx', 'head'), may hold values from -6 to 6
- softmax_value: bfloat16 [2048, 1024], P('ctx', 'head'), may hold values from -6 to 6
- document_ids: int32 [16], P('ctx'), may hold values from 0 to 3, never falling along the last dimension, each value on 1 to 12 neighbouring positions
- block_lists: int32 [16, 2], P('ctx'), may hold values from 0 to 2, all different within a row
- linear_key: bfloat16 [2048, 1024], P('ctx', 'head'), may hold values from -0.5 to 0.5
- linear_value: bfloat16 [2048, 1024], P('ctx', 'head'), may hold values from -6 to 6
- linear_decay: float32 [8, 2048], P('head', 'ctx'), may hold values from -0.7 to 0
- linear_gain: float32 [1024], P('head'), may hold values from 0.5 to 1.5
- linear_cotangent: bfloat16 [2048, 1024], P('ctx', 'head'), may hold values from -6 to 6
Outputs:
- softmax_output: bfloat16 [2048, 1024], P('ctx', 'head')
- softmax_query_grad: bfloat16 [2048, 1024], P('ctx', 'head')
- softmax_key_grad: bfloat16 [2048, 1024], P('ctx', 'head')
- softmax_value_grad: bfloat16 [2048, 1024], P('ctx', 'head')
- linear_output: bfloat16 [2048, 1024], P('ctx', 'head')
- linear_query_grad: bfloat16 [2048, 1024], P('ctx', 'head')
- linear_key_grad: bfloat16 [2048, 1024], P('ctx', 'head')
- linear_value_grad: bfloat16 [2048, 1024], P('ctx', 'head')
The draws below stay inside these ranges and needn't reach their ends.
Inputs may be any that keep to these rules, and one draw needn't show every extreme that they name: `document_ids`: never falls from block to block; a document covers 1 to 12 blocks. `block_lists`: the entries of a row are distinct.
All inputs are finite; a program needn't handle non-finite values.
Results may differ from the reference program's by a relative error of at most 0.04.
Values may be sent and summed in bfloat16 or wider, within the bound.
A program may use at most 64 MiB of HBM per device.

```python
import math
import jax
import jax.numpy as jnp
import numpy as np
from jax import lax

HD = 128
BLK = 128
WB = 4
KSEL = 2
NUM_ATTN_GROUPS = 8
T_DEV = 128
WORD_SPAN_SIZE = 2048
NBLK = 16
N_CTX = 16


def attention_pair(key):
    extent = (WORD_SPAN_SIZE, NUM_ATTN_GROUPS * HD)
    first = jax.random.fold_in(key, 101)
    latter_member = jax.random.fold_in(key, 102)
    queries = jnp.clip(jax.random.normal(first, extent, jnp.float32), -6.0, 6.0)
    keys_drawn = jnp.clip(jax.random.normal(latter_member, extent, jnp.float32), -6.0, 6.0)
    return (queries.astype(jnp.bfloat16), keys_drawn.astype(jnp.bfloat16))


def draw_softmax_query(key, part):
    return attention_pair(key)[0]


def draw_softmax_key(key, part):
    return attention_pair(key)[1]


def draw_linear_decay(key, part):
    key_heads = jax.random.fold_in(key, 301)
    key_spans = jax.random.fold_in(key, 302)
    key_cells = jax.random.fold_in(key, 303)
    key_positions = jax.random.fold_in(key, 304)
    retrieval_extra_weights = jax.random.fold_in(key, 305)
    quick_share = 0.5
    quick_heads = jax.random.uniform(key_heads, (NUM_ATTN_GROUPS, 1), jnp.float32) < quick_share
    baseline = jnp.where(quick_heads, -1.0 / 40.0, -0.3 / WORD_SPAN_SIZE)
    span_factor = jnp.exp(jax.random.uniform(key_spans, (NUM_ATTN_GROUPS, NBLK, 1), jnp.float32, -0.69, 0.69))
    span_factor = jnp.broadcast_to(span_factor, (NUM_ATTN_GROUPS, NBLK, BLK)).reshape(NUM_ATTN_GROUPS, WORD_SPAN_SIZE)
    cell_factor = jnp.exp(jax.random.uniform(key_cells, (NUM_ATTN_GROUPS, WORD_SPAN_SIZE), jnp.float32, -0.35, 0.35))
    forgetting_factor_list = baseline * span_factor * cell_factor
    spike_positions = jax.random.randint(key_positions, (NUM_ATTN_GROUPS, 2), 0, WORD_SPAN_SIZE)
    flurry_occurrences = jnp.any(jnp.arange(WORD_SPAN_SIZE)[None, :, None] == spike_positions[:, None, :], axis=2)
    flurry_extra_weight = jnp.log(jax.random.uniform(retrieval_extra_weights, (NUM_ATTN_GROUPS, WORD_SPAN_SIZE), jnp.float32, 0.5, 0.8))
    return jnp.where(flurry_occurrences, flurry_extra_weight, forgetting_factor_list).astype(jnp.float32)


def levels(stream_key, dims, pieces, smallest, largest):
    def one(axis_at, parts):
        draws = jax.random.uniform(jax.random.fold_in(jax.random.fold_in(stream_key, 6), axis_at), (parts,), jnp.float32, smallest / len(pieces), largest / len(pieces))
        return jnp.repeat(jnp.exp(draws), dims[axis_at] // parts).reshape((-1,) + (1,) * (len(dims) - axis_at - 1))

    level = one(*pieces[0])
    for cut in pieces[1:]:
        level = level * one(*cut)
    return level


def choose_distinct(rng, rows, number_of, top, lift):
    sequence = jax.random.permutation(jax.random.fold_in(rng, 1), number_of)
    boost = sequence
    for power in range(3):
        boost = boost * boost // number_of
    boost = boost * lift // number_of
    tickets = jax.random.randint(jax.random.fold_in(rng, 2), (rows, number_of), 0, 4096) + boost
    fixed_rows = jax.random.permutation(jax.random.fold_in(rng, 3), rows)[jnp.arange(number_of) % rows]
    tickets = jnp.where(jnp.arange(rows)[:, None] == fixed_rows[None, :], 1 << 14, tickets)
    score = tickets * number_of + jnp.arange(number_of)
    return lax.top_k(score.astype(jnp.int32), top)[1].astype(jnp.int32)


def profile(number_of, total, bound, skew):
    loads = [(1 << 20) // math.isqrt(grade ** skew) + 1 for grade in range(2, number_of + 1)]
    surplus, holding = total - bound - (number_of - 1), [1] * (number_of - 1)
    while surplus > 0:
        candidates = [i for i in range(number_of - 1) if holding[i] < bound]
        whole, left = sum([loads[i] for i in candidates]), surplus
        for i in candidates:
            addition = min(bound - holding[i], max(1, left * loads[i] // whole), surplus)
            holding[i] = holding[i] + addition
            surplus = surplus - addition
    return np.array([bound] + holding)


def ragged(own_key, amount, total, reach, lean):
    if amount == 2:
        one = jax.random.randint(own_key, (), max(1, total - reach), min(reach, total - 1) + 1)
        return jnp.stack([one, total - one])
    sizes = jnp.asarray(profile(amount, total, reach, lean), jnp.int32)
    pairs = (amount - 1) // 2
    source_of, taker = sizes[1:1 + 2 * pairs:2], sizes[2:2 + 2 * pairs:2]
    room = jnp.minimum(source_of - 1, reach - taker)
    moved = jax.random.randint(jax.random.fold_in(own_key, 1), (pairs,), 0, 1 << 20) % (room + 1)
    sizes = sizes.at[1:1 + 2 * pairs:2].set(source_of - moved).at[2:2 + 2 * pairs:2].set(taker + moved)
    return sizes[jax.random.permutation(jax.random.fold_in(own_key, 2), amount)]


def bell_draw(rng, shape, deviation, limit, pieces=(), held_as=jnp.bfloat16):
    level = levels(rng, shape, pieces, -0.22, 0.18) if pieces else 1.0
    drawn = jax.random.normal(rng, shape, jnp.float32) * deviation * level
    return jnp.minimum(jnp.maximum(drawn, -limit), limit).astype(held_as)


def setup_inputs(seed: int = 0) -> dict:
    key_of = jax.random.split(jax.random.key(seed), 11)
    softmax_query = draw_softmax_query(jax.random.fold_in(key_of[10], 71), 0)
    softmax_key = draw_softmax_key(jax.random.fold_in(key_of[10], 71), 0)
    softmax_value = bell_draw(key_of[2], (WORD_SPAN_SIZE, NUM_ATTN_GROUPS * HD), 1.0, 6.0, ((0, 16), (1, 2)))
    document_ids = jnp.searchsorted(jnp.cumsum(ragged(key_of[3], NBLK // 4, NBLK, 12, 1)), jnp.arange(NBLK), side="right").astype(jnp.int32)
    block_lists = choose_distinct(key_of[4], NBLK, WB - 1, KSEL, 0)
    linear_key = bell_draw(key_of[5], (WORD_SPAN_SIZE, NUM_ATTN_GROUPS * HD), HD ** -0.5, 0.5, ((0, 16), (1, 2)))
    linear_value = bell_draw(key_of[6], (WORD_SPAN_SIZE, NUM_ATTN_GROUPS * HD), 1.0, 6.0, ((0, 16), (1, 2)))
    linear_decay = draw_linear_decay(jax.random.fold_in(key_of[10], 71), 0)
    linear_gain = jnp.clip(1.0 + 0.1 * jax.random.normal(key_of[8], (NUM_ATTN_GROUPS * HD,), jnp.float32), 0.5, 1.5)
    linear_cotangent = bell_draw(key_of[9], (WORD_SPAN_SIZE, NUM_ATTN_GROUPS * HD), 1.0, 6.0, ((0, 16), (1, 2)))
    return {"softmax_query": softmax_query, "softmax_key": softmax_key, "softmax_value": softmax_value, "document_ids": document_ids, "block_lists": block_lists, "linear_key": linear_key, "linear_value": linear_value, "linear_decay": linear_decay, "linear_gain": linear_gain, "linear_cotangent": linear_cotangent}


NEG_FILL = -1e+30
EPSILON = 1e-05

def token_visible(query_blocks, lookup_segments, query_docs, key_docs, query_lists, block_total):
    offsets = query_blocks[:, None] - lookup_segments[None, :]
    listed = jnp.any(query_lists[:, :, None] + 1 == offsets[:, None, :], axis=1)
    inside = (lookup_segments >= 0) & (lookup_segments < block_total)
    inside_query = (query_blocks >= 0) & (query_blocks < block_total)
    allowed = inside_query[:, None] & inside[None, :] & (query_docs[:, None] == key_docs[None, :]) & ((offsets == 0) | listed)
    expanded = jnp.repeat(jnp.repeat(allowed, BLK, axis=0), BLK, axis=1)
    within = jnp.arange(BLK, dtype=jnp.int32)
    asking_items = (query_blocks[:, None] * BLK + within[None, :]).reshape(-1)
    key_tokens = (lookup_segments[:, None] * BLK + within[None, :]).reshape(-1)
    return expanded & (asking_items[:, None] >= key_tokens[None, :])

def tile_forward(query_rows, key_rows, value_rows, visible):
    scaling = 1.0 / math.sqrt(query_rows.shape[-1])
    scores = jnp.einsum('bnhd,bmhd->bhnm', query_rows.astype(jnp.float32), key_rows.astype(jnp.float32)) * scaling
    scores = jnp.where(visible[:, None], scores, NEG_FILL)
    row_max = lax.optimization_barrier(jnp.max(scores, axis=-1))
    raised = jnp.exp(scores - row_max[..., None])
    row_sum = lax.optimization_barrier(jnp.sum(raised, axis=-1))
    weights = (raised / row_sum[..., None]).astype(jnp.bfloat16)
    output = jnp.einsum('bhnm,bmhd->bnhd', weights.astype(jnp.float32), value_rows.astype(jnp.float32))
    return (output, row_max + jnp.log(row_sum))

def tile_backward(query_rows, key_rows, value_rows, visible, cotangent, logsum, deltas):
    scaling = 1.0 / math.sqrt(query_rows.shape[-1])
    query_float = query_rows.astype(jnp.float32)
    key_float = key_rows.astype(jnp.float32)
    value_float = value_rows.astype(jnp.float32)
    cot_float = cotangent.astype(jnp.float32)
    scores = jnp.einsum('bnhd,bmhd->bhnm', query_float, key_float) * scaling
    chances = jnp.where(visible[:, None], jnp.exp(scores - logsum[..., None]), 0.0)
    rounded = chances.astype(jnp.bfloat16).astype(jnp.float32)
    value_grad = jnp.einsum('bhnm,bnhd->bmhd', rounded, cot_float)
    chance_grad = jnp.einsum('bnhd,bmhd->bhnm', cot_float, value_float)
    score_grad = (chances * (chance_grad - deltas[..., None])).astype(jnp.bfloat16).astype(jnp.float32)
    query_grad = jnp.einsum('bhnm,bmhd->bnhd', score_grad, key_float) * scaling
    key_grad = jnp.einsum('bhnm,bnhd->bmhd', score_grad, query_float) * scaling
    return (query_grad, key_grad, value_grad)

def padded_inputs(key_input, value_input, document_ids):
    margin = WB - 1
    padding = jnp.zeros((margin * BLK, NUM_ATTN_GROUPS, HD), jnp.bfloat16)
    padded_keys = jnp.concatenate([padding, key_input.reshape(WORD_SPAN_SIZE, NUM_ATTN_GROUPS, HD)], axis=0)
    padded_values = jnp.concatenate([padding, value_input.reshape(WORD_SPAN_SIZE, NUM_ATTN_GROUPS, HD)], axis=0)
    padded_docs = jnp.concatenate([jnp.full((margin,), -1, jnp.int32), document_ids.astype(jnp.int32)], axis=0)
    return (padded_keys, padded_values, padded_docs)

def block_window(padded_keys, padded_values, padded_docs, document_ids, block_lists, block_index):
    margin = WB - 1
    offsets = jnp.arange(WB, dtype=jnp.int32)
    row_start = (block_index * BLK).astype(jnp.int32)
    window_keys = lax.dynamic_slice_in_dim(padded_keys, row_start, WB * BLK, 0)
    window_values = lax.dynamic_slice_in_dim(padded_values, row_start, WB * BLK, 0)
    window_docs = lax.dynamic_slice_in_dim(padded_docs, block_index.astype(jnp.int32), WB, 0)
    lookup_segments = block_index - margin + offsets
    visible = token_visible(block_index[None], lookup_segments, document_ids[block_index][None], window_docs, block_lists[block_index][None], NBLK)
    return (row_start, window_keys, window_values, visible)

def softmax_forward(queries, key_input, value_input, document_ids, block_lists):
    padded_keys, padded_values, padded_docs = padded_inputs(key_input, value_input, document_ids)
    query_blocks = queries.reshape(NBLK, BLK, NUM_ATTN_GROUPS, HD)

    def visit(carry, block_index):
        row_start, window_keys, window_values, visible = block_window(padded_keys, padded_values, padded_docs, document_ids, block_lists, block_index)
        output, logsum = tile_forward(query_blocks[block_index][None], window_keys[None], window_values[None], visible[None])
        return (carry, (output[0].astype(jnp.bfloat16), logsum[0]))
    unused, (outputs, logsums) = lax.scan(visit, jnp.zeros((), jnp.float32), jnp.arange(NBLK, dtype=jnp.int32))
    return (outputs.reshape(WORD_SPAN_SIZE, NUM_ATTN_GROUPS * HD), logsums)

def softmax_backward(queries, key_input, value_input, cotangent, document_ids, block_lists, outputs, logsums):
    margin = WB - 1
    padded_keys, padded_values, padded_docs = padded_inputs(key_input, value_input, document_ids)
    query_blocks = queries.reshape(NBLK, BLK, NUM_ATTN_GROUPS, HD)
    cot_blocks = cotangent.reshape(NBLK, BLK, NUM_ATTN_GROUPS, HD)
    out_blocks = outputs.reshape(NBLK, BLK, NUM_ATTN_GROUPS, HD)

    def visit(carry, block_index):
        key_acc, value_acc = carry
        row_start, window_keys, window_values, visible = block_window(padded_keys, padded_values, padded_docs, document_ids, block_lists, block_index)
        query_tile = query_blocks[block_index][None]
        cot_tile = cot_blocks[block_index][None]
        out_tile = out_blocks[block_index][None]
        deltas = lax.optimization_barrier(jnp.sum(cot_tile.astype(jnp.float32) * out_tile.astype(jnp.float32), axis=-1)).transpose(0, 2, 1)
        query_grad, key_grad, value_grad = tile_backward(query_tile, window_keys[None], window_values[None], visible[None], cot_tile, logsums[block_index][None], deltas)
        key_acc = lax.dynamic_update_slice_in_dim(key_acc, lax.dynamic_slice_in_dim(key_acc, row_start, WB * BLK, 0) + key_grad[0], row_start, 0)
        value_acc = lax.dynamic_update_slice_in_dim(value_acc, lax.dynamic_slice_in_dim(value_acc, row_start, WB * BLK, 0) + value_grad[0], row_start, 0)
        return ((key_acc, value_acc), query_grad[0].astype(jnp.bfloat16))
    zero_grads = jnp.zeros(((NBLK + margin) * BLK, NUM_ATTN_GROUPS, HD), jnp.float32)
    carried, produced = lax.scan(visit, (zero_grads, zero_grads), jnp.arange(NBLK, dtype=jnp.int32))
    flat_shape = (WORD_SPAN_SIZE, NUM_ATTN_GROUPS * HD)
    key_total = carried[0][margin * BLK:].astype(jnp.bfloat16).reshape(flat_shape)
    summed_vector_entry = carried[1][margin * BLK:].astype(jnp.bfloat16).reshape(flat_shape)
    return (produced.reshape(flat_shape), key_total, summed_vector_entry)

def to_half(values):
    return lax.optimization_barrier(values.astype(jnp.bfloat16)).astype(jnp.float32)

def stretch_parts(query_span, key_span, rate_span):
    running = jnp.cumsum(rate_span, axis=1)
    length = rate_span.shape[1]
    order = jnp.arange(length, dtype=jnp.int32)
    causal = (order[:, None] >= order[None, :])[None]
    spread = running[:, :, None] - running[:, None, :]
    damping = jnp.where(causal, jnp.exp(jnp.where(causal, spread, 0.0)), 0.0)
    products = jnp.einsum('thd,jhd->htj', query_span.astype(jnp.float32), key_span.astype(jnp.float32))
    mixing = (products * damping).astype(jnp.bfloat16)
    to_end = jnp.exp(running[:, -1:] - running)
    carry_out = jnp.exp(running[:, -1])
    return (running, damping, mixing, to_end, carry_out)

def linear_layer(queries, key_input, value_input, decay, gain, cotangent):
    spans = N_CTX
    span_shape = (spans, T_DEV, NUM_ATTN_GROUPS, HD)
    query_all = queries.reshape(span_shape)
    key_all = key_input.reshape(span_shape)
    value_all = value_input.reshape(span_shape)
    rate_all = decay.reshape(NUM_ATTN_GROUPS, spans, T_DEV).transpose(1, 0, 2)
    gain_rows = gain.reshape(NUM_ATTN_GROUPS, HD)
    features = NUM_ATTN_GROUPS * HD

    def forward(state_in, operand_bundle):
        query_span, key_span, value_span, rate_span = operand_bundle
        running, damping, mixing, to_end, carry_out = stretch_parts(query_span, key_span, rate_span)
        inner = jnp.einsum('htj,jhd->thd', mixing.astype(jnp.float32), value_span.astype(jnp.float32))
        decay_in = jnp.exp(running).T[:, :, None]
        state_half = to_half(state_in)
        raw_output = inner + decay_in * jnp.einsum('thd,hde->the', query_span.astype(jnp.float32), state_half)
        keys_scaled = to_half(key_span.astype(jnp.float32) * to_end.T[:, :, None])
        update = jnp.einsum('jhd,jhe->hde', keys_scaled, value_span.astype(jnp.float32))
        return (carry_out[:, None, None] * state_in + update, (raw_output, state_in))
    initial = jnp.zeros((NUM_ATTN_GROUPS, HD, HD), jnp.float32)
    unused, (raws, states) = lax.scan(forward, initial, (query_all, key_all, value_all, rate_all))
    squares = lax.optimization_barrier(jnp.sum(raws * raws, axis=(2, 3)))
    root_mean = jnp.sqrt(squares / features + EPSILON)
    output = (raws / root_mean[..., None, None] * gain_rows).astype(jnp.bfloat16)
    scaled = cotangent.reshape(span_shape).astype(jnp.float32) * gain_rows
    dot_sums = lax.optimization_barrier(jnp.sum(scaled * raws, axis=(2, 3)))
    raw_grads = (scaled - raws * (dot_sums / (features * root_mean * root_mean))[..., None, None]) / root_mean[..., None, None]

    def backward(later_grad, operand_bundle):
        query_span, key_span, value_span, rate_span, state_in, grad_span = operand_bundle
        running, damping, mixing, to_end, carry_out = stretch_parts(query_span, key_span, rate_span)
        query_float = query_span.astype(jnp.float32)
        key_float = key_span.astype(jnp.float32)
        value_float = value_span.astype(jnp.float32)
        grad_half = to_half(grad_span)
        state_half = to_half(state_in)
        later_half = to_half(later_grad)
        decay_in = jnp.exp(running).T[:, :, None]
        leave_factor = to_end.T[:, :, None]
        mix_grad = (jnp.einsum('thd,jhd->htj', grad_half, value_float) * damping).astype(jnp.bfloat16).astype(jnp.float32)
        query_grad = jnp.einsum('htj,jhd->thd', mix_grad, key_float) + decay_in * jnp.einsum('the,hde->thd', grad_half, state_half)
        key_grad = jnp.einsum('htj,thd->jhd', mix_grad, query_float) + leave_factor * jnp.einsum('jhe,hde->jhd', value_float, later_half)
        value_grad = jnp.einsum('htj,thd->jhd', mixing.astype(jnp.float32), grad_half) + leave_factor * jnp.einsum('jhd,hde->jhe', key_float, later_half)
        queries_scaled = to_half(query_float * decay_in)
        earlier = carry_out[:, None, None] * later_grad + jnp.einsum('thd,the->hde', queries_scaled, grad_half)
        return (earlier, (query_grad.astype(jnp.bfloat16), key_grad.astype(jnp.bfloat16), value_grad.astype(jnp.bfloat16)))
    unused_two, grads_out = lax.scan(backward, initial, (query_all, key_all, value_all, rate_all, states, raw_grads), reverse=True)
    flat_shape = (WORD_SPAN_SIZE, NUM_ATTN_GROUPS * HD)
    return (output.reshape(flat_shape), grads_out[0].reshape(flat_shape), grads_out[1].reshape(flat_shape), grads_out[2].reshape(flat_shape))

def reference(softmax_query, softmax_key, softmax_value, document_ids, block_lists, linear_key, linear_value, linear_decay, linear_gain, linear_cotangent):
    softmax_output, logsums = softmax_forward(softmax_query, softmax_key, softmax_value, document_ids, block_lists)
    linear_parts = linear_layer(softmax_output, linear_key, linear_value, linear_decay, linear_gain, linear_cotangent)
    soft_grads = softmax_backward(softmax_query, softmax_key, softmax_value, linear_parts[1], document_ids, block_lists, softmax_output, logsums)
    return (softmax_output, soft_grads[0], soft_grads[1], soft_grads[2], linear_parts[0], linear_parts[1], linear_parts[2], linear_parts[3])
```

```python
import functools
import math

import jax
import jax.numpy as jnp
from jax import lax
from jax.experimental import pallas as pl
from jax.experimental.pallas import tpu as pltpu
from jax.sharding import PartitionSpec as P

HD = 128
BLK = 128
REACH = 3
NEG = -1e30
EPSILON = 1e-05
MESH = pl.DeviceIdType.MESH
F32 = jnp.float32
BF16 = jnp.bfloat16


def dot(a, b, contract, precision=None):
    return lax.dot_general(
        a, b, (contract, ((), ())), precision=precision, preferred_element_type=F32
    )


def nn(a, b):
    return dot(a, b, ((1,), (0,)))


def nt(a, b):
    return dot(a, b, ((1,), (1,)))


def tn(a, b):
    return dot(a, b, ((0,), (0,)))


def kernel(
    n,
    groups,
    q_ref,
    k_ref,
    v_ref,
    doc_ref,
    list_ref,
    lk_ref,
    lv_ref,
    decay_ref,
    gain_ref,
    cot_ref,
    out_ref,
    dq_ref,
    dk_ref,
    dv_ref,
    lout_ref,
    lqg_ref,
    lkg_ref,
    lvg_ref,
    kbuf,
    vbuf,
    qbuf,
    gbuf,
    info,
    info_left,
    info_right,
    side,
    sidebuf,
    score,
    up_send,
    up_recv,
    state_send,
    state_recv,
    back_send,
    back_recv,
    later_send,
    later_recv,
    sums,
    sums_recv,
    near_send,
    near_recv,
    far_send,
    far_recv,
    head_send,
    head_recv,
):
    me = lax.axis_index("ctx")
    group = lax.axis_index("head")
    heads = q_ref.shape[1] // HD
    rows = heads * HD // n
    scaling = 1.0 / math.sqrt(HD)
    cols = [slice(h * HD, (h + 1) * HD) for h in range(heads)]

    barrier = pltpu.get_barrier_semaphore()

    def greet(o, c):
        pl.semaphore_signal(
            barrier, inc=1, device_id={"ctx": lax.rem(me + o, n)}, device_id_type=MESH
        )
        return c

    lax.fori_loop(1, n, greet, 0)
    for o in range(1, groups):
        pl.semaphore_signal(
            barrier, inc=1, device_id={"head": lax.rem(group + o, groups)}, device_id_type=MESH
        )

    def spread(src, dst, lane):
        def one(o, c):
            j = lax.rem(me + o, n)
            pltpu.make_async_remote_copy(
                src_ref=src.at[j],
                dst_ref=dst.at[me],
                send_sem=far_send.at[lane, j],
                recv_sem=far_recv.at[lane, me],
                device_id={"ctx": j},
                device_id_type=MESH,
            ).start()
            return c

        lax.fori_loop(1, n, one, 0)
        dst[me] = src[me]

    def collect(src, dst, lane):
        def one(o, c):
            j = lax.rem(me + n - o, n)
            pltpu.make_async_remote_copy(
                src_ref=src.at[j],
                dst_ref=dst.at[j],
                send_sem=far_send.at[lane, j],
                recv_sem=far_recv.at[lane, j],
                device_id={"ctx": j},
                device_id_type=MESH,
            ).wait()
            return c

        lax.fori_loop(1, n, one, 0)

    def near(kind, d, src, dst, step):
        return pltpu.make_async_remote_copy(
            src_ref=src,
            dst_ref=dst.at[d],
            send_sem=near_send.at[kind, d],
            recv_sem=near_recv.at[kind, d],
            device_id={"ctx": lax.rem(me + step + n, n)},
            device_id_type=MESH,
        )

    def send_near(kind, src, dst, way):
        for d in range(1, REACH + 1):
            target = me + way * d

            @pl.when((target >= 0) & (target < n))
            def _():
                near(kind, d, src, dst, way * d).start()

    def wait_near(kind, src, dst, way):
        for d in range(1, REACH + 1):
            target = me + way * d
            source = me - way * d

            @pl.when((target >= 0) & (target < n))
            def _():
                near(kind, d, src, dst, way * d).wait_send()

            @pl.when((source >= 0) & (source < n))
            def _():
                near(kind, d, src, dst, way * d).wait_recv()

    row_at = lax.broadcasted_iota(jnp.int32, (BLK, BLK), 0)
    col_at = lax.broadcasted_iota(jnp.int32, (BLK, BLK), 1)
    lower = (row_at >= col_at).astype(F32)
    rates = decay_ref[...]
    exact = lax.Precision.HIGHEST
    run_col = dot(lower, rates, ((1,), (1,)), exact)
    run_row = dot(rates, lower, ((1,), (1,)), exact)
    last = dot(rates, jnp.ones((BLK, BLK), F32), ((1,), (0,)), exact)
    carry = jnp.exp(last)
    causal = row_at >= col_at

    at_col = [jnp.broadcast_to(run_col[:, h : h + 1], (BLK, HD)) for h in range(heads)]
    leave = [jnp.exp(last[h : h + 1, :] - at_col[h]) for h in range(heads)]
    enter = [jnp.exp(at_col[h]) for h in range(heads)]
    damping = [
        jnp.where(causal, jnp.exp(jnp.where(causal, at_col[h] - run_row[h : h + 1, :], 0.0)), 0.0)
        for h in range(heads)
    ]
    updates = [
        tn((lk_ref[:, cols[h]].astype(F32) * leave[h]).astype(BF16), lv_ref[:, cols[h]])
        for h in range(heads)
    ]
    ext = up_send.shape[1] - rows
    high = carry.astype(BF16).astype(F32)
    low = carry - high
    ext_at = lax.broadcasted_iota(jnp.int32, (ext, HD), 0)
    tails = [
        jnp.where(ext_at < ext // 2, high[h : h + 1, :], low[h : h + 1, :]) for h in range(heads)
    ]
    per_head = n // heads
    for h in range(heads):
        for j in range(per_head):
            piece = jnp.concatenate([updates[h][j * rows : (j + 1) * rows], tails[h]], axis=0)
            up_send[h * per_head + j] = piece.astype(BF16)

    doc = doc_ref[0].astype(F32)
    first = list_ref[0, 0].astype(F32)
    second = list_ref[0, 1].astype(F32)
    info_at = lax.broadcasted_iota(jnp.int32, (8, HD), 0)
    info[...] = jnp.where(info_at == 0, doc, jnp.where(info_at == 1, first, second))
    kbuf[0] = k_ref[...]
    vbuf[0] = v_ref[...]
    qbuf[0] = q_ref[...]
    for d in range(1, REACH + 1):

        @pl.when(me - d < 0)
        def _():
            kbuf[d] = jnp.zeros_like(kbuf[d])
            vbuf[d] = jnp.zeros_like(vbuf[d])
            info_left[d] = jnp.full((8, HD), -1.0, F32)

        @pl.when(me + d >= n)
        def _():
            qbuf[d] = jnp.zeros_like(qbuf[d])
            gbuf[d] = jnp.zeros_like(gbuf[d])
            sidebuf[d] = jnp.zeros((8, HD), F32)
            info_right[d] = jnp.full((8, HD), -1.0, F32)

    pl.semaphore_wait(barrier, n - 1 + groups - 1)

    spread(up_send, up_recv, 0)
    send_near(0, info, info_left, 1)
    send_near(1, k_ref, kbuf, 1)
    send_near(2, v_ref, vbuf, 1)
    send_near(3, info, info_right, -1)

    collect(up_send, up_recv, 0)

    def carry_of(p):
        tail = up_recv[p, rows:, :].astype(F32)
        return tail[0:1, :] + tail[ext // 2 : ext // 2 + 1, :]

    def forward(p, state):
        state_send[p] = state.astype(BF16)
        return carry_of(p) * state + up_recv[p, :rows, :].astype(F32)

    lax.fori_loop(0, n, forward, jnp.zeros((rows, HD), F32))
    spread(state_send, state_recv, 1)

    wait_near(0, info, info_left, 1)
    wait_near(1, k_ref, kbuf, 1)
    bias = [jnp.where(causal, 0.0, NEG)]
    for d in range(1, REACH + 1):
        listed = (jnp.full((1, HD), first) == d - 1.0) | (jnp.full((1, HD), second) == d - 1.0)
        seen = (info_left[d][0:1, :] == doc) & listed
        bias.append(jnp.broadcast_to(jnp.where(seen, 0.0, NEG), (BLK, HD)))
    bias = jnp.concatenate(bias, axis=1)
    weights = []
    logsum = []
    for h in range(heads):
        keys = kbuf[:, :, cols[h]].reshape(-1, HD)
        s = nt(q_ref[:, cols[h]], keys) * scaling + bias
        score[h] = s
        m = jnp.max(s, axis=1, keepdims=True)
        e = jnp.exp(s - m)
        total = jnp.sum(e, axis=1, keepdims=True)
        weights.append((e / total).astype(BF16))
        logsum.append(m + jnp.log(total))
    wait_near(2, v_ref, vbuf, 1)
    send_near(4, q_ref, qbuf, -1)
    outs = []
    for h in range(heads):
        o = nn(weights[h], vbuf[:, :, cols[h]].reshape(-1, HD)).astype(BF16)
        outs.append(o)
        out_ref[:, cols[h]] = o

    mixing = [
        (nt(outs[h], lk_ref[:, cols[h]]) * damping[h]).astype(BF16) for h in range(heads)
    ]
    inner = [nn(mixing[h], lv_ref[:, cols[h]]) for h in range(heads)]
    collect(state_send, state_recv, 1)
    states = state_recv[...].astype(F32).reshape(heads * HD, HD).astype(BF16)
    raws = []
    scaled = []
    squares = jnp.zeros((BLK, HD), F32)
    cross = jnp.zeros((BLK, HD), F32)
    for h in range(heads):
        raw = inner[h] + enter[h] * nn(outs[h], states[h * HD : (h + 1) * HD])
        sc = cot_ref[:, cols[h]].astype(F32) * gain_ref[:, cols[h]]
        squares += raw * raw
        cross += sc * raw
        raws.append(raw)
        scaled.append(sc)
    sums[...] = jnp.where(
        col_at < HD // 2,
        jnp.sum(squares, axis=1, keepdims=True),
        jnp.sum(cross, axis=1, keepdims=True),
    )

    def to_head(o):
        return pltpu.make_async_remote_copy(
            src_ref=sums,
            dst_ref=sums_recv.at[o],
            send_sem=head_send.at[o],
            recv_sem=head_recv.at[o],
            device_id={"head": lax.rem(group + o, groups)},
            device_id_type=MESH,
        )

    for o in range(1, groups):
        to_head(o).start()
    qscaled = [(outs[h].astype(F32) * enter[h]).astype(BF16) for h in range(heads)]
    total = sums[...]
    for o in range(1, groups):
        to_head(o).wait()
        total = total + sums_recv[o]
    features = heads * HD * groups
    mean = jnp.broadcast_to(total[:, 0:1], (BLK, HD)) / features + EPSILON
    inverse = lax.rsqrt(mean)
    factor = jnp.broadcast_to(total[:, HD // 2 : HD // 2 + 1], (BLK, HD)) / (features * mean)
    halves = [((scaled[h] - raws[h] * factor) * inverse).astype(BF16) for h in range(heads)]
    mix_grads = []
    deltas = []
    for h in range(heads):
        mg = (nt(halves[h], lv_ref[:, cols[h]]) * damping[h]).astype(BF16)
        mix_grads.append(mg)
        g = nn(mg, lk_ref[:, cols[h]]) + enter[h] * nt(halves[h], states[h * HD : (h + 1) * HD])
        g = g.astype(BF16)
        lqg_ref[:, cols[h]] = g
        gbuf[0, :, cols[h]] = g
        deltas.append(
            jnp.sum(g.astype(F32) * outs[h].astype(F32), axis=1, keepdims=True)
        )
    block = jnp.zeros((BLK, HD), F32)
    for h in range(heads):
        block = jnp.where(col_at == h, logsum[h], block)
        block = jnp.where(col_at == heads + h, deltas[h], block)
    side[...] = block.T[0 : 2 * heads, :]
    sidebuf[0] = side[...]
    send_near(5, gbuf.at[0], gbuf, -1)
    send_near(6, side, sidebuf, -1)
    for h in range(heads):
        back = tn(qscaled[h], halves[h])
        for j in range(per_head):
            back_send[h * per_head + j] = back[j * rows : (j + 1) * rows].astype(BF16)
    spread(back_send, back_recv, 2)

    for h in range(heads):
        lout_ref[:, cols[h]] = (raws[h] * inverse * gain_ref[:, cols[h]]).astype(BF16)
    for h in range(heads):
        chance = jnp.exp(score[h] - logsum[h])
        cg = nt(gbuf[0, :, cols[h]], vbuf[:, :, cols[h]].reshape(-1, HD))
        sg = (chance * (cg - deltas[h])).astype(BF16)
        keys = kbuf[:, :, cols[h]].reshape(-1, HD)
        dq_ref[:, cols[h]] = (nn(sg, keys) * scaling).astype(BF16)

    collect(back_send, back_recv, 2)

    def backward(i, state):
        p = n - 1 - i
        later_send[p] = state.astype(BF16)
        return carry_of(p) * state + back_recv[p].astype(F32)

    lax.fori_loop(0, n, backward, jnp.zeros((rows, HD), F32))
    spread(later_send, later_recv, 3)
    key_local = [tn(mix_grads[h], outs[h]) for h in range(heads)]
    value_local = [tn(mixing[h], halves[h]) for h in range(heads)]

    wait_near(3, info, info_right, -1)
    wait_near(4, q_ref, qbuf, -1)
    bias = [jnp.where(row_at <= col_at, 0.0, NEG)]
    for d in range(1, REACH + 1):
        theirs = info_right[d]
        listed = (theirs[1:2, :] == d - 1.0) | (theirs[2:3, :] == d - 1.0)
        seen = (theirs[0:1, :] == doc) & listed
        bias.append(jnp.broadcast_to(jnp.where(seen, 0.0, NEG), (BLK, HD)))
    bias = jnp.concatenate(bias, axis=1)
    wait_near(5, gbuf.at[0], gbuf, -1)
    wait_near(6, side, sidebuf, -1)
    for h in range(heads):
        queries = qbuf[:, :, cols[h]].reshape(-1, HD)
        grads = gbuf[:, :, cols[h]].reshape(-1, HD)
        logs = jnp.concatenate([sidebuf[d, h : h + 1, :] for d in range(REACH + 1)], axis=1)
        dels = jnp.concatenate(
            [sidebuf[d, heads + h : heads + h + 1, :] for d in range(REACH + 1)], axis=1
        )
        chance = jnp.exp(nt(k_ref[:, cols[h]], queries) * scaling + bias - logs)
        dv_ref[:, cols[h]] = nn(chance.astype(BF16), grads).astype(BF16)
        cg = nt(v_ref[:, cols[h]], grads)
        sg = (chance * (cg - dels)).astype(BF16)
        dk_ref[:, cols[h]] = (nn(sg, queries) * scaling).astype(BF16)

    collect(later_send, later_recv, 3)
    laters = later_recv[...].astype(F32).reshape(heads * HD, HD).astype(BF16)
    for h in range(heads):
        later = laters[h * HD : (h + 1) * HD]
        lkg_ref[:, cols[h]] = (
            key_local[h] + leave[h] * nt(lv_ref[:, cols[h]], later)
        ).astype(BF16)
        lvg_ref[:, cols[h]] = (
            value_local[h] + leave[h] * nn(lk_ref[:, cols[h]], later)
        ).astype(BF16)


def body(
    softmax_query,
    softmax_key,
    softmax_value,
    document_ids,
    block_lists,
    linear_key,
    linear_value,
    linear_decay,
    linear_gain,
    linear_cotangent,
):
    n = lax.axis_size("ctx")
    groups = lax.axis_size("head")
    length, width = softmax_query.shape
    heads = width // HD
    rows = heads * HD // n
    ext = 16 if rows % 16 == 0 else 8
    vmem = pl.BlockSpec(memory_space=pltpu.VMEM)
    smem = pl.BlockSpec(memory_space=pltpu.SMEM)
    slots = REACH + 1
    window = pltpu.VMEM((slots, length, width), BF16)
    part = pltpu.VMEM((n, rows, HD), BF16)
    return pl.pallas_call(
        functools.partial(kernel, n, groups),
        out_shape=[jax.ShapeDtypeStruct((length, width), BF16)] * 8,
        in_specs=[vmem, vmem, vmem, smem, smem, vmem, vmem, vmem, vmem, vmem],
        out_specs=[vmem] * 8,
        scratch_shapes=[
            window,
            window,
            window,
            window,
            pltpu.VMEM((8, HD), F32),
            pltpu.VMEM((slots, 8, HD), F32),
            pltpu.VMEM((slots, 8, HD), F32),
            pltpu.VMEM((2 * heads, HD), F32),
            pltpu.VMEM((slots, 2 * heads, HD), F32),
            pltpu.VMEM((heads, length, slots * HD), F32),
            pltpu.VMEM((n, rows + ext, HD), BF16),
            pltpu.VMEM((n, rows + ext, HD), BF16),
            part,
            part,
            part,
            part,
            part,
            part,
            pltpu.VMEM((length, HD), F32),
            pltpu.VMEM((groups, length, HD), F32),
            pltpu.SemaphoreType.DMA((7, slots)),
            pltpu.SemaphoreType.DMA((7, slots)),
            pltpu.SemaphoreType.DMA((4, n)),
            pltpu.SemaphoreType.DMA((4, n)),
            pltpu.SemaphoreType.DMA((groups,)),
            pltpu.SemaphoreType.DMA((groups,)),
        ],
        compiler_params=pltpu.CompilerParams(
            collective_id=0, has_side_effects=True, vmem_limit_bytes=32 * 1024 * 1024
        ),
    )(
        softmax_query,
        softmax_key,
        softmax_value,
        document_ids,
        block_lists,
        linear_key,
        linear_value,
        linear_decay,
        linear_gain.reshape(1, width),
        linear_cotangent,
    )


def solution(mesh):
    tokens = P("ctx", "head")
    return jax.shard_map(
        body,
        mesh=mesh,
        in_specs=(
            tokens,
            tokens,
            tokens,
            P("ctx"),
            P("ctx", None),
            tokens,
            tokens,
            P("head", "ctx"),
            P("head"),
            tokens,
        ),
        out_specs=(tokens,) * 8,
        check_vma=False,
    )
```

```python
import functools
import math

import jax
import jax.numpy as jnp
from jax import lax
from jax.experimental import pallas as pl
from jax.experimental.pallas import tpu as pltpu
from jax.sharding import PartitionSpec as P

HD = 128
BLK = 128
REACH = 3
NEG = -1e30
EPSILON = 1e-05
MESH = pl.DeviceIdType.MESH
F32 = jnp.float32
BF16 = jnp.bfloat16


def dot(a, b, contract, precision=None):
    return lax.dot_general(
        a, b, (contract, ((), ())), precision=precision, preferred_element_type=F32
    )


def nn(a, b):
    return dot(a, b, ((1,), (0,)))


def nt(a, b):
    return dot(a, b, ((1,), (1,)))


def tn(a, b):
    return dot(a, b, ((0,), (0,)))


def kernel(
    n,
    groups,
    q_hbm,
    k_hbm,
    v_hbm,
    doc_hbm,
    list_hbm,
    lk_hbm,
    lv_hbm,
    decay_hbm,
    gain_hbm,
    cot_hbm,
    out_hbm,
    dq_hbm,
    dk_hbm,
    dv_hbm,
    lout_hbm,
    lqg_hbm,
    lkg_hbm,
    lvg_hbm,
    stage,
    leaving,
    doc_ref,
    list_ref,
    lk_ref,
    lv_ref,
    decay_ref,
    gain_ref,
    cot_ref,
    load,
    kbuf,
    vbuf,
    qbuf,
    gbuf,
    info,
    info_left,
    info_right,
    side,
    sidebuf,
    score,
    up_send,
    up_recv,
    state_send,
    state_recv,
    back_send,
    back_recv,
    later_send,
    later_recv,
    sums,
    sums_recv,
    near_send,
    near_recv,
    far_send,
    far_recv,
    head_send,
    head_recv,
):
    out_ref, dq_ref, dk_ref, dv_ref, lout_ref, lqg_ref, lkg_ref, lvg_ref = [
        stage.at[i] for i in range(8)
    ]
    homes = (out_hbm, dq_hbm, dk_hbm, dv_hbm, lout_hbm, lqg_hbm, lkg_hbm, lvg_hbm)
    leaves = [
        pltpu.make_async_copy(stage.at[i], homes[i], leaving.at[i]) for i in range(8)
    ]
    q_ref, k_ref, v_ref = qbuf.at[0], kbuf.at[0], vbuf.at[0]
    loads = [
        pltpu.make_async_copy(src, dst, load.at[i])
        for i, (src, dst) in enumerate(
            [
                (decay_hbm, decay_ref),
                (lk_hbm, lk_ref),
                (lv_hbm, lv_ref),
                (doc_hbm, doc_ref),
                (list_hbm, list_ref),
                (k_hbm, k_ref),
                (v_hbm, v_ref),
                (q_hbm, q_ref),
                (gain_hbm, gain_ref),
                (cot_hbm, cot_ref),
            ]
        )
    ]
    for copy in loads:
        copy.start()
    me = lax.axis_index("ctx")
    group = lax.axis_index("head")
    heads = q_hbm.shape[1] // HD
    rows = heads * HD // n
    scaling = 1.0 / math.sqrt(HD)
    cols = [slice(h * HD, (h + 1) * HD) for h in range(heads)]

    barrier = pltpu.get_barrier_semaphore()

    def greet(o, c):
        pl.semaphore_signal(
            barrier, inc=1, device_id={"ctx": lax.rem(me + o, n)}, device_id_type=MESH
        )
        return c

    lax.fori_loop(1, n, greet, 0)
    for o in range(1, groups):
        pl.semaphore_signal(
            barrier, inc=1, device_id={"head": lax.rem(group + o, groups)}, device_id_type=MESH
        )

    def spread(src, dst, lane):
        def one(o, c):
            j = lax.rem(me + o, n)
            pltpu.make_async_remote_copy(
                src_ref=src.at[j],
                dst_ref=dst.at[me],
                send_sem=far_send.at[lane, j],
                recv_sem=far_recv.at[lane, me],
                device_id={"ctx": j},
                device_id_type=MESH,
            ).start()
            return c

        lax.fori_loop(1, n, one, 0)
        dst[me] = src[me]

    def collect(src, dst, lane):
        def one(o, c):
            j = lax.rem(me + n - o, n)
            pltpu.make_async_remote_copy(
                src_ref=src.at[j],
                dst_ref=dst.at[j],
                send_sem=far_send.at[lane, j],
                recv_sem=far_recv.at[lane, j],
                device_id={"ctx": j},
                device_id_type=MESH,
            ).wait()
            return c

        lax.fori_loop(1, n, one, 0)

    def near(kind, d, src, dst, step):
        return pltpu.make_async_remote_copy(
            src_ref=src,
            dst_ref=dst.at[d],
            send_sem=near_send.at[kind, d],
            recv_sem=near_recv.at[kind, d],
            device_id={"ctx": lax.rem(me + step + n, n)},
            device_id_type=MESH,
        )

    def send_near(kind, src, dst, way):
        for d in range(1, REACH + 1):
            target = me + way * d

            @pl.when((target >= 0) & (target < n))
            def _():
                near(kind, d, src, dst, way * d).start()

    def wait_near(kind, src, dst, way):
        for d in range(1, REACH + 1):
            target = me + way * d
            source = me - way * d

            @pl.when((target >= 0) & (target < n))
            def _():
                near(kind, d, src, dst, way * d).wait_send()

            @pl.when((source >= 0) & (source < n))
            def _():
                near(kind, d, src, dst, way * d).wait_recv()

    loads[0].wait()
    row_at = lax.broadcasted_iota(jnp.int32, (BLK, BLK), 0)
    col_at = lax.broadcasted_iota(jnp.int32, (BLK, BLK), 1)
    lower = (row_at >= col_at).astype(F32)
    rates = decay_ref[...]
    exact = lax.Precision.HIGHEST
    run_col = dot(lower, rates, ((1,), (1,)), exact)
    run_row = dot(rates, lower, ((1,), (1,)), exact)
    last = dot(rates, jnp.ones((BLK, BLK), F32), ((1,), (0,)), exact)
    carry = jnp.exp(last)
    causal = row_at >= col_at

    at_col = [jnp.broadcast_to(run_col[:, h : h + 1], (BLK, HD)) for h in range(heads)]
    leave = [jnp.exp(last[h : h + 1, :] - at_col[h]) for h in range(heads)]
    enter = [jnp.exp(at_col[h]) for h in range(heads)]
    damping = [
        jnp.where(causal, jnp.exp(jnp.where(causal, at_col[h] - run_row[h : h + 1, :], 0.0)), 0.0)
        for h in range(heads)
    ]
    loads[1].wait()
    loads[2].wait()
    updates = [
        tn((lk_ref[:, cols[h]].astype(F32) * leave[h]).astype(BF16), lv_ref[:, cols[h]])
        for h in range(heads)
    ]
    ext = up_send.shape[1] - rows
    high = carry.astype(BF16).astype(F32)
    low = carry - high
    ext_at = lax.broadcasted_iota(jnp.int32, (ext, HD), 0)
    tails = [
        jnp.where(ext_at < ext // 2, high[h : h + 1, :], low[h : h + 1, :]) for h in range(heads)
    ]
    per_head = n // heads
    for h in range(heads):
        for j in range(per_head):
            piece = jnp.concatenate([updates[h][j * rows : (j + 1) * rows], tails[h]], axis=0)
            up_send[h * per_head + j] = piece.astype(BF16)

    loads[3].wait()
    loads[4].wait()
    doc = jnp.full((1, HD), doc_ref[0].astype(F32))
    first = jnp.broadcast_to(list_ref[:, 0:1].astype(F32), (1, HD))
    second = jnp.broadcast_to(list_ref[:, 1:2].astype(F32), (1, HD))
    info_at = lax.broadcasted_iota(jnp.int32, (8, HD), 0)
    info[...] = jnp.where(info_at == 0, doc, jnp.where(info_at == 1, first, second))
    for d in range(1, REACH + 1):

        @pl.when(me - d < 0)
        def _():
            kbuf[d] = jnp.zeros_like(kbuf[d])
            vbuf[d] = jnp.zeros_like(vbuf[d])
            info_left[d] = jnp.full((8, HD), -1.0, F32)

        @pl.when(me + d >= n)
        def _():
            qbuf[d] = jnp.zeros_like(qbuf[d])
            gbuf[d] = jnp.zeros_like(gbuf[d])
            sidebuf[d] = jnp.zeros((8, HD), F32)
            info_right[d] = jnp.full((8, HD), -1.0, F32)

    for copy in loads[5:]:
        copy.wait()
    pl.semaphore_wait(barrier, n - 1 + groups - 1)

    spread(up_send, up_recv, 0)
    send_near(0, info, info_left, 1)
    send_near(1, k_ref, kbuf, 1)
    send_near(2, v_ref, vbuf, 1)
    send_near(3, info, info_right, -1)

    collect(up_send, up_recv, 0)

    def carry_of(p):
        tail = up_recv[p, rows:, :].astype(F32)
        return tail[0:1, :] + tail[ext // 2 : ext // 2 + 1, :]

    def forward(p, state):
        state_send[p] = state.astype(BF16)
        return carry_of(p) * state + up_recv[p, :rows, :].astype(F32)

    lax.fori_loop(0, n, forward, jnp.zeros((rows, HD), F32))
    spread(state_send, state_recv, 1)

    wait_near(0, info, info_left, 1)
    wait_near(1, k_ref, kbuf, 1)
    bias = [jnp.where(causal, 0.0, NEG)]
    for d in range(1, REACH + 1):
        listed = (first == d - 1.0) | (second == d - 1.0)
        seen = (info_left[d][0:1, :] == doc) & listed
        bias.append(jnp.broadcast_to(jnp.where(seen, 0.0, NEG), (BLK, HD)))
    bias = jnp.concatenate(bias, axis=1)
    weights = []
    logsum = []
    for h in range(heads):
        keys = kbuf[:, :, cols[h]].reshape(-1, HD)
        s = nt(q_ref[:, cols[h]], keys) * scaling + bias
        score[h] = s
        m = jnp.max(s, axis=1, keepdims=True)
        e = jnp.exp(s - m)
        total = jnp.sum(e, axis=1, keepdims=True)
        weights.append((e / total).astype(BF16))
        logsum.append(m + jnp.log(total))
    wait_near(2, v_ref, vbuf, 1)
    send_near(4, q_ref, qbuf, -1)
    outs = []
    for h in range(heads):
        o = nn(weights[h], vbuf[:, :, cols[h]].reshape(-1, HD)).astype(BF16)
        outs.append(o)
        out_ref[:, cols[h]] = o
    leaves[0].start()

    mixing = [
        (nt(outs[h], lk_ref[:, cols[h]]) * damping[h]).astype(BF16) for h in range(heads)
    ]
    inner = [nn(mixing[h], lv_ref[:, cols[h]]) for h in range(heads)]
    collect(state_send, state_recv, 1)
    states = state_recv[...].astype(F32).reshape(heads * HD, HD).astype(BF16)
    raws = []
    scaled = []
    squares = jnp.zeros((BLK, HD), F32)
    cross = jnp.zeros((BLK, HD), F32)
    for h in range(heads):
        raw = inner[h] + enter[h] * nn(outs[h], states[h * HD : (h + 1) * HD])
        sc = cot_ref[:, cols[h]].astype(F32) * gain_ref[:, cols[h]]
        squares += raw * raw
        cross += sc * raw
        raws.append(raw)
        scaled.append(sc)
    sums[...] = jnp.where(
        col_at < HD // 2,
        jnp.sum(squares, axis=1, keepdims=True),
        jnp.sum(cross, axis=1, keepdims=True),
    )

    def to_head(o):
        return pltpu.make_async_remote_copy(
            src_ref=sums,
            dst_ref=sums_recv.at[o],
            send_sem=head_send.at[o],
            recv_sem=head_recv.at[o],
            device_id={"head": lax.rem(group + o, groups)},
            device_id_type=MESH,
        )

    for o in range(1, groups):
        to_head(o).start()
    qscaled = [(outs[h].astype(F32) * enter[h]).astype(BF16) for h in range(heads)]
    total = sums[...]
    for o in range(1, groups):
        to_head(o).wait()
        total = total + sums_recv[o]
    features = heads * HD * groups
    mean = jnp.broadcast_to(total[:, 0:1], (BLK, HD)) / features + EPSILON
    inverse = lax.rsqrt(mean)
    factor = jnp.broadcast_to(total[:, HD // 2 : HD // 2 + 1], (BLK, HD)) / (features * mean)
    halves = [((scaled[h] - raws[h] * factor) * inverse).astype(BF16) for h in range(heads)]
    for h in range(heads):
        back = tn(qscaled[h], halves[h])
        for j in range(per_head):
            back_send[h * per_head + j] = back[j * rows : (j + 1) * rows].astype(BF16)
    spread(back_send, back_recv, 2)
    mix_grads = []
    deltas = []
    for h in range(heads):
        mg = (nt(halves[h], lv_ref[:, cols[h]]) * damping[h]).astype(BF16)
        mix_grads.append(mg)
        g = nn(mg, lk_ref[:, cols[h]]) + enter[h] * nt(halves[h], states[h * HD : (h + 1) * HD])
        g = g.astype(BF16)
        lqg_ref[:, cols[h]] = g
        gbuf[0, :, cols[h]] = g
        deltas.append(
            jnp.sum(g.astype(F32) * outs[h].astype(F32), axis=1, keepdims=True)
        )
    block = jnp.zeros((BLK, HD), F32)
    for h in range(heads):
        block = jnp.where(col_at == h, logsum[h], block)
        block = jnp.where(col_at == heads + h, deltas[h], block)
    side[...] = block.T[0 : 2 * heads, :]
    sidebuf[0] = side[...]
    send_near(5, gbuf.at[0], gbuf, -1)
    send_near(6, side, sidebuf, -1)

    leaves[5].start()
    for h in range(heads):
        lout_ref[:, cols[h]] = (raws[h] * inverse * gain_ref[:, cols[h]]).astype(BF16)
    leaves[4].start()
    for h in range(heads):
        chance = jnp.exp(score[h] - logsum[h])
        cg = nt(gbuf[0, :, cols[h]], vbuf[:, :, cols[h]].reshape(-1, HD))
        sg = (chance * (cg - deltas[h])).astype(BF16)
        keys = kbuf[:, :, cols[h]].reshape(-1, HD)
        dq_ref[:, cols[h]] = (nn(sg, keys) * scaling).astype(BF16)
    leaves[1].start()

    collect(back_send, back_recv, 2)

    def backward(i, state):
        p = n - 1 - i
        later_send[p] = state.astype(BF16)
        return carry_of(p) * state + back_recv[p].astype(F32)

    lax.fori_loop(0, n, backward, jnp.zeros((rows, HD), F32))
    spread(later_send, later_recv, 3)
    key_local = [tn(mix_grads[h], outs[h]) for h in range(heads)]
    value_local = [tn(mixing[h], halves[h]) for h in range(heads)]

    wait_near(3, info, info_right, -1)
    wait_near(4, q_ref, qbuf, -1)
    bias = [jnp.where(row_at <= col_at, 0.0, NEG)]
    for d in range(1, REACH + 1):
        theirs = info_right[d]
        listed = (theirs[1:2, :] == d - 1.0) | (theirs[2:3, :] == d - 1.0)
        seen = (theirs[0:1, :] == doc) & listed
        bias.append(jnp.broadcast_to(jnp.where(seen, 0.0, NEG), (BLK, HD)))
    bias = jnp.concatenate(bias, axis=1)
    wait_near(5, gbuf.at[0], gbuf, -1)
    wait_near(6, side, sidebuf, -1)
    for h in range(heads):
        queries = qbuf[:, :, cols[h]].reshape(-1, HD)
        grads = gbuf[:, :, cols[h]].reshape(-1, HD)
        logs = jnp.concatenate([sidebuf[d, h : h + 1, :] for d in range(REACH + 1)], axis=1)
        dels = jnp.concatenate(
            [sidebuf[d, heads + h : heads + h + 1, :] for d in range(REACH + 1)], axis=1
        )
        chance = jnp.exp(nt(k_ref[:, cols[h]], queries) * scaling + bias - logs)
        dv_ref[:, cols[h]] = nn(chance.astype(BF16), grads).astype(BF16)
        cg = nt(v_ref[:, cols[h]], grads)
        sg = (chance * (cg - dels)).astype(BF16)
        dk_ref[:, cols[h]] = (nn(sg, queries) * scaling).astype(BF16)
    leaves[2].start()
    leaves[3].start()

    collect(later_send, later_recv, 3)
    laters = later_recv[...].astype(F32).reshape(heads * HD, HD).astype(BF16)
    for h in range(heads):
        later = laters[h * HD : (h + 1) * HD]
        lkg_ref[:, cols[h]] = (
            key_local[h] + leave[h] * nt(lv_ref[:, cols[h]], later)
        ).astype(BF16)
        lvg_ref[:, cols[h]] = (
            value_local[h] + leave[h] * nn(lk_ref[:, cols[h]], later)
        ).astype(BF16)
    leaves[6].start()
    leaves[7].start()
    for copy in leaves:
        copy.wait()


def store_all(*refs):
    done = refs[16]
    copies = [pltpu.make_async_copy(refs[i], refs[8 + i], done.at[i]) for i in range(8)]
    for copy in copies:
        copy.start()
    for copy in copies:
        copy.wait()


def body(
    softmax_query,
    softmax_key,
    softmax_value,
    document_ids,
    block_lists,
    linear_key,
    linear_value,
    linear_decay,
    linear_gain,
    linear_cotangent,
):
    n = lax.axis_size("ctx")
    groups = lax.axis_size("head")
    length, width = softmax_query.shape
    heads = width // HD
    rows = heads * HD // n
    ext = 16 if rows % 16 == 0 else 8
    anywhere = pl.BlockSpec(memory_space=pl.ANY)
    array = pltpu.VMEM((length, width), BF16)
    slots = REACH + 1
    window = pltpu.VMEM((slots, length, width), BF16)
    part = pltpu.VMEM((n, rows, HD), BF16)
    results = pl.pallas_call(
        functools.partial(kernel, n, groups),
        out_shape=[jax.ShapeDtypeStruct((length, width), BF16)] * 8,
        in_specs=[anywhere] * 10,
        out_specs=[anywhere] * 8,
        scratch_shapes=[
            pltpu.VMEM((8, length, width), BF16),
            pltpu.SemaphoreType.DMA((8,)),
            pltpu.SMEM((1,), jnp.int32),
            pltpu.VMEM((1, 2), jnp.int32),
            array,
            array,
            pltpu.VMEM((heads, length), F32),
            pltpu.VMEM((1, width), F32),
            array,
            pltpu.SemaphoreType.DMA((10,)),
            window,
            window,
            window,
            window,
            pltpu.VMEM((8, HD), F32),
            pltpu.VMEM((slots, 8, HD), F32),
            pltpu.VMEM((slots, 8, HD), F32),
            pltpu.VMEM((2 * heads, HD), F32),
            pltpu.VMEM((slots, 2 * heads, HD), F32),
            pltpu.VMEM((heads, length, slots * HD), F32),
            pltpu.VMEM((n, rows + ext, HD), BF16),
            pltpu.VMEM((n, rows + ext, HD), BF16),
            part,
            part,
            part,
            part,
            part,
            part,
            pltpu.VMEM((length, HD), F32),
            pltpu.VMEM((groups, length, HD), F32),
            pltpu.SemaphoreType.DMA((7, slots)),
            pltpu.SemaphoreType.DMA((7, slots)),
            pltpu.SemaphoreType.DMA((4, n)),
            pltpu.SemaphoreType.DMA((4, n)),
            pltpu.SemaphoreType.DMA((groups,)),
            pltpu.SemaphoreType.DMA((groups,)),
        ],
        compiler_params=pltpu.CompilerParams(
            collective_id=0, has_side_effects=True, vmem_limit_bytes=60 * 1024 * 1024
        ),
    )(
        softmax_query,
        softmax_key,
        softmax_value,
        document_ids,
        block_lists,
        linear_key,
        linear_value,
        linear_decay,
        linear_gain.reshape(1, width),
        linear_cotangent,
    )
    store = pl.pallas_call(
        store_all,
        out_shape=[jax.ShapeDtypeStruct((length, width), BF16)] * 8,
        in_specs=[anywhere] * 8,
        out_specs=[anywhere] * 8,
        scratch_shapes=[pltpu.SemaphoreType.DMA((8,))],
        compiler_params=pltpu.CompilerParams(vmem_limit_bytes=60 * 1024 * 1024),
    )
    return tuple(store(*results))


def solution(mesh):
    tokens = P("ctx", "head")
    return jax.shard_map(
        body,
        mesh=mesh,
        in_specs=(
            tokens,
            tokens,
            tokens,
            P("ctx"),
            P("ctx", None),
            tokens,
            tokens,
            P("head", "ctx"),
            P("head"),
            tokens,
        ),
        out_specs=(tokens,) * 8,
        check_vma=False,
    )
```

```python
import functools
import math

import jax
import jax.numpy as jnp
from jax import lax
from jax.experimental import pallas as pl
from jax.experimental.pallas import tpu as pltpu
from jax.sharding import PartitionSpec as P

HD = 128
BLK = 128
REACH = 3
GROUP = 4
NEG = -1e30
EPSILON = 1e-05
MESH = pl.DeviceIdType.MESH
F32 = jnp.float32
BF16 = jnp.bfloat16


def dot(a, b, contract, precision=None):
    return lax.dot_general(
        a, b, (contract, ((), ())), precision=precision, preferred_element_type=F32
    )


def nn(a, b):
    return dot(a, b, ((1,), (0,)))


def nt(a, b):
    return dot(a, b, ((1,), (1,)))


def tn(a, b):
    return dot(a, b, ((0,), (0,)))


def kernel(
    n,
    groups,
    q_hbm,
    k_hbm,
    v_hbm,
    doc_hbm,
    list_hbm,
    lk_hbm,
    lv_hbm,
    decay_hbm,
    gain_hbm,
    cot_hbm,
    out_hbm,
    dq_hbm,
    dk_hbm,
    dv_hbm,
    lout_hbm,
    lqg_hbm,
    lkg_hbm,
    lvg_hbm,
    stage,
    leaving,
    doc_ref,
    list_ref,
    lk_ref,
    lv_ref,
    decay_ref,
    gain_ref,
    cot_ref,
    load,
    kbuf,
    vbuf,
    qbuf,
    gbuf,
    info,
    info_left,
    info_right,
    side,
    sidebuf,
    score,
    up_send,
    up_recv,
    state_send,
    state_recv,
    back_send,
    back_recv,
    later_send,
    later_recv,
    sums,
    sums_recv,
    relayed,
    relay_send,
    relay_recv,
    near_send,
    near_recv,
    far_send,
    far_recv,
    head_send,
    head_recv,
):
    out_ref, dq_ref, dk_ref, dv_ref, lout_ref, lqg_ref, lkg_ref, lvg_ref = [
        stage.at[i] for i in range(8)
    ]
    homes = (out_hbm, dq_hbm, dk_hbm, dv_hbm, lout_hbm, lqg_hbm, lkg_hbm, lvg_hbm)
    leaves = [
        pltpu.make_async_copy(stage.at[i], homes[i], leaving.at[i]) for i in range(8)
    ]
    q_ref, k_ref, v_ref = qbuf.at[0], kbuf.at[0], vbuf.at[0]
    loads = [
        pltpu.make_async_copy(src, dst, load.at[i])
        for i, (src, dst) in enumerate(
            [
                (decay_hbm, decay_ref),
                (lk_hbm, lk_ref),
                (lv_hbm, lv_ref),
                (doc_hbm, doc_ref),
                (list_hbm, list_ref),
                (k_hbm, k_ref),
                (v_hbm, v_ref),
                (q_hbm, q_ref),
                (gain_hbm, gain_ref),
                (cot_hbm, cot_ref),
            ]
        )
    ]
    for copy in loads:
        copy.start()
    me = lax.axis_index("ctx")
    group = lax.axis_index("head")
    heads = q_hbm.shape[1] // HD
    rows = heads * HD // n
    scaling = 1.0 / math.sqrt(HD)
    cols = [slice(h * HD, (h + 1) * HD) for h in range(heads)]

    barrier = pltpu.get_barrier_semaphore()

    def greet(o, c):
        pl.semaphore_signal(
            barrier, inc=1, device_id={"ctx": lax.rem(me + o, n)}, device_id_type=MESH
        )
        return c

    lax.fori_loop(1, n, greet, 0)
    for o in range(1, groups):
        pl.semaphore_signal(
            barrier, inc=1, device_id={"head": lax.rem(group + o, groups)}, device_id_type=MESH
        )

    def spread(src, dst, lane):
        def one(o, c):
            j = lax.rem(me + o, n)
            pltpu.make_async_remote_copy(
                src_ref=src.at[j],
                dst_ref=dst.at[me],
                send_sem=far_send.at[lane, j],
                recv_sem=far_recv.at[lane, me],
                device_id={"ctx": j},
                device_id_type=MESH,
            ).start()
            return c

        lax.fori_loop(1, n, one, 0)
        dst[me] = src[me]

    def collect(src, dst, lane):
        def one(o, c):
            j = lax.rem(me + n - o, n)
            pltpu.make_async_remote_copy(
                src_ref=src.at[j],
                dst_ref=dst.at[j],
                send_sem=far_send.at[lane, j],
                recv_sem=far_recv.at[lane, j],
                device_id={"ctx": j},
                device_id_type=MESH,
            ).wait()
            return c

        lax.fori_loop(1, n, one, 0)

    def near(kind, d, src, dst, step):
        return pltpu.make_async_remote_copy(
            src_ref=src,
            dst_ref=dst.at[d],
            send_sem=near_send.at[kind, d],
            recv_sem=near_recv.at[kind, d],
            device_id={"ctx": lax.rem(me + step + n, n)},
            device_id_type=MESH,
        )

    place = lax.rem(me, GROUP)

    def send_small(kind, src, dst, way):
        for d in range(1, REACH + 1):
            target = me + way * d

            @pl.when((target >= 0) & (target < n))
            def _():
                near(kind, d, src, dst, way * d).start()

    def wait_small(kind, src, dst, way):
        for d in range(1, REACH + 1):
            target = me + way * d
            source = me - way * d

            @pl.when((target >= 0) & (target < n))
            def _():
                near(kind, d, src, dst, way * d).wait_send()

            @pl.when((source >= 0) & (source < n))
            def _():
                near(kind, d, src, dst, way * d).wait_recv()

    def ahead(way):
        return place if way > 0 else GROUP - 1 - place

    def inside(way, groups_on):
        target = me + way * GROUP * groups_on
        return (ahead(way) >= 1) & (target >= 0) & (target < n)

    def relay(kind, src, way):
        return pltpu.make_async_remote_copy(
            src_ref=src,
            dst_ref=relayed.at[kind],
            send_sem=relay_send.at[kind],
            recv_sem=relay_recv.at[kind],
            device_id={"ctx": lax.rem(me + way * GROUP + n, n)},
            device_id_type=MESH,
        )

    def send_across(kind, src, way):
        @pl.when(inside(way, 1))
        def _():
            relay(kind, src, way).start()

    def send_direct(kind, src, dst, way):
        for d in range(1, REACH + 1):

            @pl.when(ahead(way) + d < GROUP)
            def _():
                near(kind, d, src, dst, way * d).start()

    def forward_on(kind, src, dst, way):
        @pl.when(inside(way, -1))
        def _():
            relay(kind, src, way).wait_recv()
            for e in range(1, GROUP):

                @pl.when(e <= ahead(way))
                def _():
                    near(kind, GROUP - e, relayed.at[kind], dst, -way * e).start()

    def wait_block(kind, src, dst, way):
        for d in range(1, REACH + 1):
            source = me - way * d

            @pl.when((source >= 0) & (source < n))
            def _():
                near(kind, d, src, dst, way * d).wait_recv()

    def wait_sent(kind, src, dst, way):
        @pl.when(inside(way, 1))
        def _():
            relay(kind, src, way).wait_send()

        for d in range(1, REACH + 1):

            @pl.when(ahead(way) + d < GROUP)
            def _():
                near(kind, d, src, dst, way * d).wait_send()

        @pl.when(inside(way, -1))
        def _():
            for e in range(1, GROUP):

                @pl.when(e <= ahead(way))
                def _():
                    near(kind, GROUP - e, relayed.at[kind], dst, -way * e).wait_send()

    loads[0].wait()
    row_at = lax.broadcasted_iota(jnp.int32, (BLK, BLK), 0)
    col_at = lax.broadcasted_iota(jnp.int32, (BLK, BLK), 1)
    lower = (row_at >= col_at).astype(F32)
    rates = decay_ref[...]
    exact = lax.Precision.HIGHEST
    run_col = dot(lower, rates, ((1,), (1,)), exact)
    run_row = dot(rates, lower, ((1,), (1,)), exact)
    last = dot(rates, jnp.ones((BLK, BLK), F32), ((1,), (0,)), exact)
    carry = jnp.exp(last)
    causal = row_at >= col_at

    at_col = [jnp.broadcast_to(run_col[:, h : h + 1], (BLK, HD)) for h in range(heads)]
    leave = [jnp.exp(last[h : h + 1, :] - at_col[h]) for h in range(heads)]
    enter = [jnp.exp(at_col[h]) for h in range(heads)]
    damping = [
        jnp.where(causal, jnp.exp(jnp.where(causal, at_col[h] - run_row[h : h + 1, :], 0.0)), 0.0)
        for h in range(heads)
    ]
    loads[1].wait()
    loads[2].wait()
    updates = [
        tn((lk_ref[:, cols[h]].astype(F32) * leave[h]).astype(BF16), lv_ref[:, cols[h]])
        for h in range(heads)
    ]
    ext = up_send.shape[1] - rows
    high = carry.astype(BF16).astype(F32)
    low = carry - high
    ext_at = lax.broadcasted_iota(jnp.int32, (ext, HD), 0)
    tails = [
        jnp.where(ext_at < ext // 2, high[h : h + 1, :], low[h : h + 1, :]) for h in range(heads)
    ]
    per_head = n // heads
    for h in range(heads):
        for j in range(per_head):
            piece = jnp.concatenate([updates[h][j * rows : (j + 1) * rows], tails[h]], axis=0)
            up_send[h * per_head + j] = piece.astype(BF16)

    loads[3].wait()
    loads[4].wait()
    doc = jnp.full((1, HD), doc_ref[0].astype(F32))
    first = jnp.broadcast_to(list_ref[:, 0:1].astype(F32), (1, HD))
    second = jnp.broadcast_to(list_ref[:, 1:2].astype(F32), (1, HD))
    info_at = lax.broadcasted_iota(jnp.int32, (8, HD), 0)
    info[...] = jnp.where(info_at == 0, doc, jnp.where(info_at == 1, first, second))
    for d in range(1, REACH + 1):

        @pl.when(me - d < 0)
        def _():
            kbuf[d] = jnp.zeros_like(kbuf[d])
            vbuf[d] = jnp.zeros_like(vbuf[d])
            info_left[d] = jnp.full((8, HD), -1.0, F32)

        @pl.when(me + d >= n)
        def _():
            qbuf[d] = jnp.zeros_like(qbuf[d])
            gbuf[d] = jnp.zeros_like(gbuf[d])
            sidebuf[d] = jnp.zeros((8, HD), F32)
            info_right[d] = jnp.full((8, HD), -1.0, F32)

    for copy in loads[5:]:
        copy.wait()
    pl.semaphore_wait(barrier, n - 1 + groups - 1)

    spread(up_send, up_recv, 0)
    send_across(1, k_ref, 1)
    send_small(0, info, info_left, 1)
    send_direct(1, k_ref, kbuf, 1)
    send_across(2, v_ref, 1)
    send_across(4, q_ref, -1)
    send_direct(2, v_ref, vbuf, 1)
    send_small(3, info, info_right, -1)

    collect(up_send, up_recv, 0)

    def carry_of(p):
        tail = up_recv[p, rows:, :].astype(F32)
        return tail[0:1, :] + tail[ext // 2 : ext // 2 + 1, :]

    def forward(p, state):
        state_send[p] = state.astype(BF16)
        return carry_of(p) * state + up_recv[p, :rows, :].astype(F32)

    lax.fori_loop(0, n, forward, jnp.zeros((rows, HD), F32))
    spread(state_send, state_recv, 1)

    forward_on(1, k_ref, kbuf, 1)
    forward_on(2, v_ref, vbuf, 1)
    wait_small(0, info, info_left, 1)
    wait_block(1, k_ref, kbuf, 1)
    bias = [jnp.where(causal, 0.0, NEG)]
    for d in range(1, REACH + 1):
        listed = (first == d - 1.0) | (second == d - 1.0)
        seen = (info_left[d][0:1, :] == doc) & listed
        bias.append(jnp.broadcast_to(jnp.where(seen, 0.0, NEG), (BLK, HD)))
    bias = jnp.concatenate(bias, axis=1)
    weights = []
    logsum = []
    for h in range(heads):
        keys = kbuf[:, :, cols[h]].reshape(-1, HD)
        s = nt(q_ref[:, cols[h]], keys) * scaling + bias
        score[h] = s
        m = jnp.max(s, axis=1, keepdims=True)
        e = jnp.exp(s - m)
        total = jnp.sum(e, axis=1, keepdims=True)
        weights.append((e / total).astype(BF16))
        logsum.append(m + jnp.log(total))
    wait_block(2, v_ref, vbuf, 1)
    send_direct(4, q_ref, qbuf, -1)
    forward_on(4, q_ref, qbuf, -1)
    outs = []
    for h in range(heads):
        o = nn(weights[h], vbuf[:, :, cols[h]].reshape(-1, HD)).astype(BF16)
        outs.append(o)
        out_ref[:, cols[h]] = o
    leaves[0].start()

    mixing = [
        (nt(outs[h], lk_ref[:, cols[h]]) * damping[h]).astype(BF16) for h in range(heads)
    ]
    inner = [nn(mixing[h], lv_ref[:, cols[h]]) for h in range(heads)]
    collect(state_send, state_recv, 1)
    states = state_recv[...].astype(F32).reshape(heads * HD, HD).astype(BF16)
    raws = []
    scaled = []
    squares = jnp.zeros((BLK, HD), F32)
    cross = jnp.zeros((BLK, HD), F32)
    for h in range(heads):
        raw = inner[h] + enter[h] * nn(outs[h], states[h * HD : (h + 1) * HD])
        sc = cot_ref[:, cols[h]].astype(F32) * gain_ref[:, cols[h]]
        squares += raw * raw
        cross += sc * raw
        raws.append(raw)
        scaled.append(sc)
    sums[...] = jnp.where(
        col_at < HD // 2,
        jnp.sum(squares, axis=1, keepdims=True),
        jnp.sum(cross, axis=1, keepdims=True),
    )

    def to_head(o):
        return pltpu.make_async_remote_copy(
            src_ref=sums,
            dst_ref=sums_recv.at[o],
            send_sem=head_send.at[o],
            recv_sem=head_recv.at[o],
            device_id={"head": lax.rem(group + o, groups)},
            device_id_type=MESH,
        )

    for o in range(1, groups):
        to_head(o).start()
    qscaled = [(outs[h].astype(F32) * enter[h]).astype(BF16) for h in range(heads)]
    total = sums[...]
    for o in range(1, groups):
        to_head(o).wait()
        total = total + sums_recv[o]
    features = heads * HD * groups
    mean = jnp.broadcast_to(total[:, 0:1], (BLK, HD)) / features + EPSILON
    inverse = lax.rsqrt(mean)
    factor = jnp.broadcast_to(total[:, HD // 2 : HD // 2 + 1], (BLK, HD)) / (features * mean)
    halves = [((scaled[h] - raws[h] * factor) * inverse).astype(BF16) for h in range(heads)]
    for h in range(heads):
        back = tn(qscaled[h], halves[h])
        for j in range(per_head):
            back_send[h * per_head + j] = back[j * rows : (j + 1) * rows].astype(BF16)
    spread(back_send, back_recv, 2)
    mix_grads = []
    deltas = []
    for h in range(heads):
        mg = (nt(halves[h], lv_ref[:, cols[h]]) * damping[h]).astype(BF16)
        mix_grads.append(mg)
        g = nn(mg, lk_ref[:, cols[h]]) + enter[h] * nt(halves[h], states[h * HD : (h + 1) * HD])
        g = g.astype(BF16)
        lqg_ref[:, cols[h]] = g
        gbuf[0, :, cols[h]] = g
        deltas.append(
            jnp.sum(g.astype(F32) * outs[h].astype(F32), axis=1, keepdims=True)
        )
    block = jnp.zeros((BLK, HD), F32)
    for h in range(heads):
        block = jnp.where(col_at == h, logsum[h], block)
        block = jnp.where(col_at == heads + h, deltas[h], block)
    side[...] = block.T[0 : 2 * heads, :]
    sidebuf[0] = side[...]
    send_across(5, gbuf.at[0], -1)
    send_direct(5, gbuf.at[0], gbuf, -1)
    send_small(6, side, sidebuf, -1)

    leaves[5].start()
    for h in range(heads):
        lout_ref[:, cols[h]] = (raws[h] * inverse * gain_ref[:, cols[h]]).astype(BF16)
    leaves[4].start()
    for h in range(heads):
        chance = jnp.exp(score[h] - logsum[h])
        cg = nt(gbuf[0, :, cols[h]], vbuf[:, :, cols[h]].reshape(-1, HD))
        sg = (chance * (cg - deltas[h])).astype(BF16)
        keys = kbuf[:, :, cols[h]].reshape(-1, HD)
        dq_ref[:, cols[h]] = (nn(sg, keys) * scaling).astype(BF16)
    leaves[1].start()
    forward_on(5, gbuf.at[0], gbuf, -1)

    collect(back_send, back_recv, 2)

    def backward(i, state):
        p = n - 1 - i
        later_send[p] = state.astype(BF16)
        return carry_of(p) * state + back_recv[p].astype(F32)

    lax.fori_loop(0, n, backward, jnp.zeros((rows, HD), F32))
    spread(later_send, later_recv, 3)
    key_local = [tn(mix_grads[h], outs[h]) for h in range(heads)]
    value_local = [tn(mixing[h], halves[h]) for h in range(heads)]

    wait_small(3, info, info_right, -1)
    wait_block(4, q_ref, qbuf, -1)
    bias = [jnp.where(row_at <= col_at, 0.0, NEG)]
    for d in range(1, REACH + 1):
        theirs = info_right[d]
        listed = (theirs[1:2, :] == d - 1.0) | (theirs[2:3, :] == d - 1.0)
        seen = (theirs[0:1, :] == doc) & listed
        bias.append(jnp.broadcast_to(jnp.where(seen, 0.0, NEG), (BLK, HD)))
    bias = jnp.concatenate(bias, axis=1)
    wait_block(5, gbuf.at[0], gbuf, -1)
    wait_small(6, side, sidebuf, -1)
    for h in range(heads):
        queries = qbuf[:, :, cols[h]].reshape(-1, HD)
        grads = gbuf[:, :, cols[h]].reshape(-1, HD)
        logs = jnp.concatenate([sidebuf[d, h : h + 1, :] for d in range(REACH + 1)], axis=1)
        dels = jnp.concatenate(
            [sidebuf[d, heads + h : heads + h + 1, :] for d in range(REACH + 1)], axis=1
        )
        chance = jnp.exp(nt(k_ref[:, cols[h]], queries) * scaling + bias - logs)
        dv_ref[:, cols[h]] = nn(chance.astype(BF16), grads).astype(BF16)
        cg = nt(v_ref[:, cols[h]], grads)
        sg = (chance * (cg - dels)).astype(BF16)
        dk_ref[:, cols[h]] = (nn(sg, queries) * scaling).astype(BF16)
    leaves[2].start()
    leaves[3].start()

    collect(later_send, later_recv, 3)
    laters = later_recv[...].astype(F32).reshape(heads * HD, HD).astype(BF16)
    for h in range(heads):
        later = laters[h * HD : (h + 1) * HD]
        lkg_ref[:, cols[h]] = (
            key_local[h] + leave[h] * nt(lv_ref[:, cols[h]], later)
        ).astype(BF16)
        lvg_ref[:, cols[h]] = (
            value_local[h] + leave[h] * nn(lk_ref[:, cols[h]], later)
        ).astype(BF16)
    leaves[6].start()
    leaves[7].start()
    wait_sent(1, k_ref, kbuf, 1)
    wait_sent(2, v_ref, vbuf, 1)
    wait_sent(4, q_ref, qbuf, -1)
    wait_sent(5, gbuf.at[0], gbuf, -1)
    for copy in leaves:
        copy.wait()


def store_all(*refs):
    held, arrived, done = refs[16:]
    loads = [pltpu.make_async_copy(refs[i], held.at[i], arrived.at[i]) for i in range(8)]
    stores = [pltpu.make_async_copy(held.at[i], refs[8 + i], done.at[i]) for i in range(8)]
    for load in loads:
        load.start()
    for load, store in zip(loads, stores):
        load.wait()
        store.start()
    for store in stores:
        store.wait()


def body(
    softmax_query,
    softmax_key,
    softmax_value,
    document_ids,
    block_lists,
    linear_key,
    linear_value,
    linear_decay,
    linear_gain,
    linear_cotangent,
):
    n = lax.axis_size("ctx")
    groups = lax.axis_size("head")
    length, width = softmax_query.shape
    heads = width // HD
    rows = heads * HD // n
    ext = 16 if rows % 16 == 0 else 8
    anywhere = pl.BlockSpec(memory_space=pl.ANY)
    array = pltpu.VMEM((length, width), BF16)
    slots = REACH + 1
    window = pltpu.VMEM((slots, length, width), BF16)
    part = pltpu.VMEM((n, rows, HD), BF16)
    results = pl.pallas_call(
        functools.partial(kernel, n, groups),
        out_shape=[jax.ShapeDtypeStruct((length, width), BF16)] * 8,
        in_specs=[anywhere] * 10,
        out_specs=[anywhere] * 8,
        scratch_shapes=[
            pltpu.VMEM((8, length, width), BF16),
            pltpu.SemaphoreType.DMA((8,)),
            pltpu.SMEM((1,), jnp.int32),
            pltpu.VMEM((1, 2), jnp.int32),
            array,
            array,
            pltpu.VMEM((heads, length), F32),
            pltpu.VMEM((1, width), F32),
            array,
            pltpu.SemaphoreType.DMA((10,)),
            window,
            window,
            window,
            window,
            pltpu.VMEM((8, HD), F32),
            pltpu.VMEM((slots, 8, HD), F32),
            pltpu.VMEM((slots, 8, HD), F32),
            pltpu.VMEM((2 * heads, HD), F32),
            pltpu.VMEM((slots, 2 * heads, HD), F32),
            pltpu.VMEM((heads, length, slots * HD), F32),
            pltpu.VMEM((n, rows + ext, HD), BF16),
            pltpu.VMEM((n, rows + ext, HD), BF16),
            part,
            part,
            part,
            part,
            part,
            part,
            pltpu.VMEM((length, HD), F32),
            pltpu.VMEM((groups, length, HD), F32),
            pltpu.VMEM((6, length, width), BF16),
            pltpu.SemaphoreType.DMA((6,)),
            pltpu.SemaphoreType.DMA((6,)),
            pltpu.SemaphoreType.DMA((7, slots)),
            pltpu.SemaphoreType.DMA((7, slots)),
            pltpu.SemaphoreType.DMA((4, n)),
            pltpu.SemaphoreType.DMA((4, n)),
            pltpu.SemaphoreType.DMA((groups,)),
            pltpu.SemaphoreType.DMA((groups,)),
        ],
        compiler_params=pltpu.CompilerParams(
            collective_id=0, has_side_effects=True, vmem_limit_bytes=60 * 1024 * 1024
        ),
    )(
        softmax_query,
        softmax_key,
        softmax_value,
        document_ids,
        block_lists,
        linear_key,
        linear_value,
        linear_decay,
        linear_gain.reshape(1, width),
        linear_cotangent,
    )
    store = pl.pallas_call(
        store_all,
        out_shape=[jax.ShapeDtypeStruct((length, width), BF16)] * 8,
        in_specs=[anywhere] * 8,
        out_specs=[anywhere] * 8,
        scratch_shapes=[
            pltpu.VMEM((8, length, width), BF16),
            pltpu.SemaphoreType.DMA((8,)),
            pltpu.SemaphoreType.DMA((8,)),
        ],
        compiler_params=pltpu.CompilerParams(vmem_limit_bytes=60 * 1024 * 1024),
    )
    return tuple(store(*results))


def solution(mesh):
    tokens = P("ctx", "head")
    return jax.shard_map(
        body,
        mesh=mesh,
        in_specs=(
            tokens,
            tokens,
            tokens,
            P("ctx"),
            P("ctx", None),
            tokens,
            tokens,
            P("head", "ctx"),
            P("head"),
            tokens,
        ),
        out_specs=(tokens,) * 8,
        check_vma=False,
    )
```

```python
import functools
import math

import jax
import jax.numpy as jnp
from jax import lax
from jax.experimental import pallas as pl
from jax.experimental.pallas import tpu as pltpu
from jax.sharding import PartitionSpec as P

HD = 128
BLK = 128
REACH = 3
GROUP = 4
NEG = -1e30
EPSILON = 1e-05
MESH = pl.DeviceIdType.MESH
F32 = jnp.float32
BF16 = jnp.bfloat16


def dot(a, b, contract, precision=None):
    return lax.dot_general(
        a, b, (contract, ((), ())), precision=precision, preferred_element_type=F32
    )


def nn(a, b):
    return dot(a, b, ((1,), (0,)))


def nt(a, b):
    return dot(a, b, ((1,), (1,)))


def tn(a, b):
    return dot(a, b, ((0,), (0,)))


def kernel(
    n,
    groups,
    q_hbm,
    k_hbm,
    v_hbm,
    doc_hbm,
    list_hbm,
    lk_hbm,
    lv_hbm,
    decay_hbm,
    gain_hbm,
    cot_hbm,
    out_hbm,
    dq_hbm,
    dk_hbm,
    dv_hbm,
    lout_hbm,
    lqg_hbm,
    lkg_hbm,
    lvg_hbm,
    stage,
    leaving,
    doc_ref,
    list_ref,
    lk_ref,
    lv_ref,
    decay_ref,
    gain_ref,
    cot_ref,
    load,
    kbuf,
    vbuf,
    qbuf,
    gbuf,
    info,
    info_left,
    info_right,
    side,
    sidebuf,
    logs_out,
    logsbuf,
    score,
    up_send,
    up_recv,
    state_send,
    state_recv,
    back_send,
    back_recv,
    later_send,
    later_recv,
    sums,
    sums_recv,
    relayed,
    relay_send,
    relay_recv,
    near_send,
    near_recv,
    far_send,
    far_recv,
    head_send,
    head_recv,
):
    out_ref, dq_ref, dk_ref, dv_ref, lout_ref, lqg_ref, lkg_ref, lvg_ref = [
        stage.at[i] for i in range(8)
    ]
    homes = (out_hbm, dq_hbm, dk_hbm, dv_hbm, lout_hbm, lqg_hbm, lkg_hbm, lvg_hbm)
    leaves = [
        pltpu.make_async_copy(stage.at[i], homes[i], leaving.at[i]) for i in range(8)
    ]
    q_ref, k_ref, v_ref = qbuf.at[0], kbuf.at[0], vbuf.at[0]
    loads = [
        pltpu.make_async_copy(src, dst, load.at[i])
        for i, (src, dst) in enumerate(
            [
                (k_hbm, k_ref),
                (v_hbm, v_ref),
                (q_hbm, q_ref),
                (decay_hbm, decay_ref),
                (lk_hbm, lk_ref),
                (lv_hbm, lv_ref),
                (doc_hbm, doc_ref),
                (list_hbm, list_ref),
                (gain_hbm, gain_ref),
                (cot_hbm, cot_ref),
            ]
        )
    ]
    for copy in loads:
        copy.start()
    me = lax.axis_index("ctx")
    group = lax.axis_index("head")
    heads = q_hbm.shape[1] // HD
    rows = heads * HD // n
    scaling = 1.0 / math.sqrt(HD)
    cols = [slice(h * HD, (h + 1) * HD) for h in range(heads)]

    barrier = pltpu.get_barrier_semaphore()

    def greet(o, c):
        pl.semaphore_signal(
            barrier, inc=1, device_id={"ctx": lax.rem(me + o, n)}, device_id_type=MESH
        )
        return c

    lax.fori_loop(1, n, greet, 0)
    for o in range(1, groups):
        pl.semaphore_signal(
            barrier, inc=1, device_id={"head": lax.rem(group + o, groups)}, device_id_type=MESH
        )

    def spread(src, dst, lane):
        def one(o, c):
            j = lax.rem(me + o, n)
            pltpu.make_async_remote_copy(
                src_ref=src.at[j],
                dst_ref=dst.at[me],
                send_sem=far_send.at[lane, j],
                recv_sem=far_recv.at[lane, me],
                device_id={"ctx": j},
                device_id_type=MESH,
            ).start()
            return c

        lax.fori_loop(1, n, one, 0)
        dst[me] = src[me]

    def collect(src, dst, lane):
        def one(o, c):
            j = lax.rem(me + n - o, n)
            pltpu.make_async_remote_copy(
                src_ref=src.at[j],
                dst_ref=dst.at[j],
                send_sem=far_send.at[lane, j],
                recv_sem=far_recv.at[lane, j],
                device_id={"ctx": j},
                device_id_type=MESH,
            ).wait()
            return c

        lax.fori_loop(1, n, one, 0)

    def near(kind, d, src, dst, step):
        return pltpu.make_async_remote_copy(
            src_ref=src,
            dst_ref=dst.at[d],
            send_sem=near_send.at[kind, d],
            recv_sem=near_recv.at[kind, d],
            device_id={"ctx": lax.rem(me + step + n, n)},
            device_id_type=MESH,
        )

    place = lax.rem(me, GROUP)

    def send_small(kind, src, dst, way):
        for d in range(1, REACH + 1):
            target = me + way * d

            @pl.when((target >= 0) & (target < n))
            def _():
                near(kind, d, src, dst, way * d).start()

    def wait_small(kind, src, dst, way):
        for d in range(1, REACH + 1):
            target = me + way * d
            source = me - way * d

            @pl.when((target >= 0) & (target < n))
            def _():
                near(kind, d, src, dst, way * d).wait_send()

            @pl.when((source >= 0) & (source < n))
            def _():
                near(kind, d, src, dst, way * d).wait_recv()

    def ahead(way):
        return place if way > 0 else GROUP - 1 - place

    def inside(way, groups_on):
        target = me + way * GROUP * groups_on
        return (ahead(way) >= 1) & (target >= 0) & (target < n)

    def relay(kind, src, way):
        return pltpu.make_async_remote_copy(
            src_ref=src,
            dst_ref=relayed.at[kind],
            send_sem=relay_send.at[kind],
            recv_sem=relay_recv.at[kind],
            device_id={"ctx": lax.rem(me + way * GROUP + n, n)},
            device_id_type=MESH,
        )

    def send_across(kind, src, way):
        @pl.when(inside(way, 1))
        def _():
            relay(kind, src, way).start()

    def send_direct(kind, src, dst, way):
        for d in range(1, REACH + 1):

            @pl.when(ahead(way) + d < GROUP)
            def _():
                near(kind, d, src, dst, way * d).start()

    def forward_on(kind, src, dst, way):
        @pl.when(inside(way, -1))
        def _():
            relay(kind, src, way).wait_recv()
            for e in range(1, GROUP):

                @pl.when(e <= ahead(way))
                def _():
                    near(kind, GROUP - e, relayed.at[kind], dst, -way * e).start()

    def wait_block(kind, src, dst, way):
        for d in range(1, REACH + 1):
            source = me - way * d

            @pl.when((source >= 0) & (source < n))
            def _():
                near(kind, d, src, dst, way * d).wait_recv()

    def wait_sent(kind, src, dst, way):
        @pl.when(inside(way, 1))
        def _():
            relay(kind, src, way).wait_send()

        for d in range(1, REACH + 1):

            @pl.when(ahead(way) + d < GROUP)
            def _():
                near(kind, d, src, dst, way * d).wait_send()

        @pl.when(inside(way, -1))
        def _():
            for e in range(1, GROUP):

                @pl.when(e <= ahead(way))
                def _():
                    near(kind, GROUP - e, relayed.at[kind], dst, -way * e).wait_send()

    loads[0].wait()
    loads[1].wait()
    pl.semaphore_wait(barrier, n - 1 + groups - 1)
    send_across(1, k_ref, 1)
    send_direct(1, k_ref, kbuf, 1)
    send_across(2, v_ref, 1)
    send_direct(2, v_ref, vbuf, 1)
    loads[2].wait()
    send_across(4, q_ref, -1)

    loads[3].wait()
    row_at = lax.broadcasted_iota(jnp.int32, (BLK, BLK), 0)
    col_at = lax.broadcasted_iota(jnp.int32, (BLK, BLK), 1)
    lower = (row_at >= col_at).astype(F32)
    rates = decay_ref[...]
    exact = lax.Precision.HIGHEST
    run_col = dot(lower, rates, ((1,), (1,)), exact)
    run_row = dot(rates, lower, ((1,), (1,)), exact)
    last = dot(rates, jnp.ones((BLK, BLK), F32), ((1,), (0,)), exact)
    carry = jnp.exp(last)
    causal = row_at >= col_at

    at_col = [jnp.broadcast_to(run_col[:, h : h + 1], (BLK, HD)) for h in range(heads)]
    leave = [jnp.exp(last[h : h + 1, :] - at_col[h]) for h in range(heads)]
    enter = [jnp.exp(at_col[h]) for h in range(heads)]
    damping = [
        jnp.where(causal, jnp.exp(jnp.where(causal, at_col[h] - run_row[h : h + 1, :], 0.0)), 0.0)
        for h in range(heads)
    ]
    loads[4].wait()
    loads[5].wait()
    updates = [
        tn((lk_ref[:, cols[h]].astype(F32) * leave[h]).astype(BF16), lv_ref[:, cols[h]])
        for h in range(heads)
    ]
    ext = up_send.shape[1] - rows
    high = carry.astype(BF16).astype(F32)
    low = carry - high
    ext_at = lax.broadcasted_iota(jnp.int32, (ext, HD), 0)
    tails = [
        jnp.where(ext_at < ext // 2, high[h : h + 1, :], low[h : h + 1, :]) for h in range(heads)
    ]
    per_head = n // heads
    for h in range(heads):
        for j in range(per_head):
            piece = jnp.concatenate([updates[h][j * rows : (j + 1) * rows], tails[h]], axis=0)
            up_send[h * per_head + j] = piece.astype(BF16)

    loads[6].wait()
    loads[7].wait()
    doc = jnp.full((1, HD), doc_ref[0].astype(F32))
    first = jnp.broadcast_to(list_ref[:, 0:1].astype(F32), (1, HD))
    second = jnp.broadcast_to(list_ref[:, 1:2].astype(F32), (1, HD))
    info_at = lax.broadcasted_iota(jnp.int32, (8, HD), 0)
    info[...] = jnp.where(info_at == 0, doc, jnp.where(info_at == 1, first, second))
    for d in range(1, REACH + 1):

        @pl.when(me - d < 0)
        def _():
            kbuf[d] = jnp.zeros_like(kbuf[d])
            vbuf[d] = jnp.zeros_like(vbuf[d])
            info_left[d] = jnp.full((8, HD), -1.0, F32)

        @pl.when(me + d >= n)
        def _():
            qbuf[d] = jnp.zeros_like(qbuf[d])
            gbuf[d] = jnp.zeros_like(gbuf[d])
            sidebuf[d] = jnp.zeros((2 * heads, HD), F32)
            logsbuf[d] = jnp.zeros((2 * heads, HD), F32)
            info_right[d] = jnp.full((8, HD), -1.0, F32)

    send_small(0, info, info_left, 1)
    send_small(3, info, info_right, -1)
    forward_on(1, k_ref, kbuf, 1)
    spread(up_send, up_recv, 0)
    forward_on(2, v_ref, vbuf, 1)

    collect(up_send, up_recv, 0)

    def carry_of(p):
        tail = up_recv[p, rows:, :].astype(F32)
        return tail[0:1, :] + tail[ext // 2 : ext // 2 + 1, :]

    def forward(p, state):
        state_send[p] = state.astype(BF16)
        return carry_of(p) * state + up_recv[p, :rows, :].astype(F32)

    lax.fori_loop(0, n, forward, jnp.zeros((rows, HD), F32))
    spread(state_send, state_recv, 1)

    wait_small(0, info, info_left, 1)
    wait_block(1, k_ref, kbuf, 1)
    bias = [jnp.where(causal, 0.0, NEG)]
    for d in range(1, REACH + 1):
        listed = (first == d - 1.0) | (second == d - 1.0)
        seen = (info_left[d][0:1, :] == doc) & listed
        bias.append(jnp.broadcast_to(jnp.where(seen, 0.0, NEG), (BLK, HD)))
    bias = jnp.concatenate(bias, axis=1)
    weights = []
    logsum = []
    for h in range(heads):
        keys = kbuf[:, :, cols[h]].reshape(-1, HD)
        s = nt(q_ref[:, cols[h]], keys) * scaling + bias
        score[h] = s
        m = jnp.max(s, axis=1, keepdims=True)
        e = jnp.exp(s - m)
        total = jnp.sum(e, axis=1, keepdims=True)
        weights.append((e * (1.0 / total)).astype(BF16))
        logsum.append(m + jnp.log(total))
    block = jnp.zeros((BLK, HD), F32)
    for h in range(heads):
        block = jnp.where(col_at == h, logsum[h], block)
    logs_out[...] = block.T[0 : 2 * heads, :]
    logsbuf[0] = logs_out[...]
    send_small(7, logs_out, logsbuf, -1)
    wait_block(2, v_ref, vbuf, 1)
    send_direct(4, q_ref, qbuf, -1)
    forward_on(4, q_ref, qbuf, -1)
    loads[8].wait()
    loads[9].wait()
    outs = []
    for h in range(heads):
        o = nn(weights[h], vbuf[:, :, cols[h]].reshape(-1, HD)).astype(BF16)
        outs.append(o)
        out_ref[:, cols[h]] = o
    leaves[0].start()

    mixing = [
        (nt(outs[h], lk_ref[:, cols[h]]) * damping[h]).astype(BF16) for h in range(heads)
    ]
    inner = [nn(mixing[h], lv_ref[:, cols[h]]) for h in range(heads)]
    collect(state_send, state_recv, 1)
    states = state_recv[...].astype(F32).reshape(heads * HD, HD).astype(BF16)
    raws = []
    scaled = []
    squares = jnp.zeros((BLK, HD), F32)
    cross = jnp.zeros((BLK, HD), F32)
    for h in range(heads):
        raw = inner[h] + enter[h] * nn(outs[h], states[h * HD : (h + 1) * HD])
        sc = cot_ref[:, cols[h]].astype(F32) * gain_ref[:, cols[h]]
        squares += raw * raw
        cross += sc * raw
        raws.append(raw)
        scaled.append(sc)
    sums[...] = jnp.where(
        col_at < HD // 2,
        jnp.sum(squares, axis=1, keepdims=True),
        jnp.sum(cross, axis=1, keepdims=True),
    )

    def to_head(o):
        return pltpu.make_async_remote_copy(
            src_ref=sums,
            dst_ref=sums_recv.at[o],
            send_sem=head_send.at[o],
            recv_sem=head_recv.at[o],
            device_id={"head": lax.rem(group + o, groups)},
            device_id_type=MESH,
        )

    for o in range(1, groups):
        to_head(o).start()
    qscaled = [(outs[h].astype(F32) * enter[h]).astype(BF16) for h in range(heads)]
    total = sums[...]
    for o in range(1, groups):
        to_head(o).wait()
        total = total + sums_recv[o]
    features = heads * HD * groups
    mean = jnp.broadcast_to(total[:, 0:1], (BLK, HD)) / features + EPSILON
    inverse = lax.rsqrt(mean)
    factor = jnp.broadcast_to(total[:, HD // 2 : HD // 2 + 1], (BLK, HD)) / (features * mean)
    halves = [((scaled[h] - raws[h] * factor) * inverse).astype(BF16) for h in range(heads)]
    mix_grads = []
    deltas = []
    gs = []
    for h in range(heads):
        mg = (nt(halves[h], lv_ref[:, cols[h]]) * damping[h]).astype(BF16)
        mix_grads.append(mg)
        g = nn(mg, lk_ref[:, cols[h]]) + enter[h] * nt(halves[h], states[h * HD : (h + 1) * HD])
        g = g.astype(BF16)
        lqg_ref[:, cols[h]] = g
        gbuf[0, :, cols[h]] = g
        gs.append(g)
    send_across(5, gbuf.at[0], -1)
    send_direct(5, gbuf.at[0], gbuf, -1)
    for h in range(heads):
        g = gs[h]
        deltas.append(
            jnp.sum(g.astype(F32) * outs[h].astype(F32), axis=1, keepdims=True)
        )
    block = jnp.zeros((BLK, HD), F32)
    for h in range(heads):
        block = jnp.where(col_at == h, deltas[h], block)
    side[...] = block.T[0 : 2 * heads, :]
    sidebuf[0] = side[...]
    send_small(6, side, sidebuf, -1)
    for h in range(heads):
        back = tn(qscaled[h], halves[h])
        for j in range(per_head):
            back_send[h * per_head + j] = back[j * rows : (j + 1) * rows].astype(BF16)
    spread(back_send, back_recv, 2)

    leaves[5].start()
    for h in range(heads):
        lout_ref[:, cols[h]] = (raws[h] * inverse * gain_ref[:, cols[h]]).astype(BF16)
    leaves[4].start()
    for h in range(heads):
        chance = jnp.exp(score[h] - logsum[h])
        cg = nt(gbuf[0, :, cols[h]], vbuf[:, :, cols[h]].reshape(-1, HD))
        sg = (chance * (cg - deltas[h])).astype(BF16)
        keys = kbuf[:, :, cols[h]].reshape(-1, HD)
        dq_ref[:, cols[h]] = (nn(sg, keys) * scaling).astype(BF16)
    leaves[1].start()
    forward_on(5, gbuf.at[0], gbuf, -1)

    collect(back_send, back_recv, 2)

    def backward(i, state):
        p = n - 1 - i
        later_send[p] = state.astype(BF16)
        return carry_of(p) * state + back_recv[p].astype(F32)

    lax.fori_loop(0, n, backward, jnp.zeros((rows, HD), F32))
    spread(later_send, later_recv, 3)
    key_local = [tn(mix_grads[h], outs[h]) for h in range(heads)]
    value_local = [tn(mixing[h], halves[h]) for h in range(heads)]

    wait_small(3, info, info_right, -1)
    wait_block(4, q_ref, qbuf, -1)
    bias = [jnp.where(row_at <= col_at, 0.0, NEG)]
    for d in range(1, REACH + 1):
        theirs = info_right[d]
        listed = (theirs[1:2, :] == d - 1.0) | (theirs[2:3, :] == d - 1.0)
        seen = (theirs[0:1, :] == doc) & listed
        bias.append(jnp.broadcast_to(jnp.where(seen, 0.0, NEG), (BLK, HD)))
    bias = jnp.concatenate(bias, axis=1)
    wait_small(7, logs_out, logsbuf, -1)
    for h in range(heads):
        queries = qbuf[:, :, cols[h]].reshape(-1, HD)
        logs = jnp.concatenate([logsbuf[d, h : h + 1, :] for d in range(REACH + 1)], axis=1)
        score[h] = jnp.exp(nt(k_ref[:, cols[h]], queries) * scaling + bias - logs)
    wait_block(5, gbuf.at[0], gbuf, -1)
    wait_small(6, side, sidebuf, -1)
    for h in range(heads):
        queries = qbuf[:, :, cols[h]].reshape(-1, HD)
        grads = gbuf[:, :, cols[h]].reshape(-1, HD)
        dels = jnp.concatenate(
            [sidebuf[d, h : h + 1, :] for d in range(REACH + 1)], axis=1
        )
        chance = score[h]
        dv_ref[:, cols[h]] = nn(chance.astype(BF16), grads).astype(BF16)
        cg = nt(v_ref[:, cols[h]], grads)
        sg = (chance * (cg - dels)).astype(BF16)
        dk_ref[:, cols[h]] = (nn(sg, queries) * scaling).astype(BF16)
    leaves[2].start()
    leaves[3].start()

    collect(later_send, later_recv, 3)
    laters = later_recv[...].astype(F32).reshape(heads * HD, HD).astype(BF16)
    for h in range(heads):
        later = laters[h * HD : (h + 1) * HD]
        lkg_ref[:, cols[h]] = (
            key_local[h] + leave[h] * nt(lv_ref[:, cols[h]], later)
        ).astype(BF16)
        lvg_ref[:, cols[h]] = (
            value_local[h] + leave[h] * nn(lk_ref[:, cols[h]], later)
        ).astype(BF16)
    leaves[6].start()
    leaves[7].start()
    wait_sent(1, k_ref, kbuf, 1)
    wait_sent(2, v_ref, vbuf, 1)
    wait_sent(4, q_ref, qbuf, -1)
    wait_sent(5, gbuf.at[0], gbuf, -1)
    for copy in leaves:
        copy.wait()


def store_all(*refs):
    held, arrived, done = refs[16:]
    loads = [pltpu.make_async_copy(refs[i], held.at[i], arrived.at[i]) for i in range(8)]
    stores = [pltpu.make_async_copy(held.at[i], refs[8 + i], done.at[i]) for i in range(8)]
    for load in loads:
        load.start()
    for load, store in zip(loads, stores):
        load.wait()
        store.start()
    for store in stores:
        store.wait()


def body(
    softmax_query,
    softmax_key,
    softmax_value,
    document_ids,
    block_lists,
    linear_key,
    linear_value,
    linear_decay,
    linear_gain,
    linear_cotangent,
):
    n = lax.axis_size("ctx")
    groups = lax.axis_size("head")
    length, width = softmax_query.shape
    heads = width // HD
    rows = heads * HD // n
    ext = 16 if rows % 16 == 0 else 8
    anywhere = pl.BlockSpec(memory_space=pl.ANY)
    array = pltpu.VMEM((length, width), BF16)
    slots = REACH + 1
    window = pltpu.VMEM((slots, length, width), BF16)
    part = pltpu.VMEM((n, rows, HD), BF16)
    results = pl.pallas_call(
        functools.partial(kernel, n, groups),
        out_shape=[jax.ShapeDtypeStruct((length, width), BF16)] * 8,
        in_specs=[anywhere] * 10,
        out_specs=[anywhere] * 8,
        scratch_shapes=[
            pltpu.VMEM((8, length, width), BF16),
            pltpu.SemaphoreType.DMA((8,)),
            pltpu.SMEM((1,), jnp.int32),
            pltpu.VMEM((1, 2), jnp.int32),
            array,
            array,
            pltpu.VMEM((heads, length), F32),
            pltpu.VMEM((1, width), F32),
            array,
            pltpu.SemaphoreType.DMA((10,)),
            window,
            window,
            window,
            window,
            pltpu.VMEM((8, HD), F32),
            pltpu.VMEM((slots, 8, HD), F32),
            pltpu.VMEM((slots, 8, HD), F32),
            pltpu.VMEM((2 * heads, HD), F32),
            pltpu.VMEM((slots, 2 * heads, HD), F32),
            pltpu.VMEM((2 * heads, HD), F32),
            pltpu.VMEM((slots, 2 * heads, HD), F32),
            pltpu.VMEM((heads, length, slots * HD), F32),
            pltpu.VMEM((n, rows + ext, HD), BF16),
            pltpu.VMEM((n, rows + ext, HD), BF16),
            part,
            part,
            part,
            part,
            part,
            part,
            pltpu.VMEM((length, HD), F32),
            pltpu.VMEM((groups, length, HD), F32),
            pltpu.VMEM((6, length, width), BF16),
            pltpu.SemaphoreType.DMA((6,)),
            pltpu.SemaphoreType.DMA((6,)),
            pltpu.SemaphoreType.DMA((8, slots)),
            pltpu.SemaphoreType.DMA((8, slots)),
            pltpu.SemaphoreType.DMA((4, n)),
            pltpu.SemaphoreType.DMA((4, n)),
            pltpu.SemaphoreType.DMA((groups,)),
            pltpu.SemaphoreType.DMA((groups,)),
        ],
        compiler_params=pltpu.CompilerParams(
            collective_id=0, has_side_effects=True, vmem_limit_bytes=60 * 1024 * 1024
        ),
    )(
        softmax_query,
        softmax_key,
        softmax_value,
        document_ids,
        block_lists,
        linear_key,
        linear_value,
        linear_decay,
        linear_gain.reshape(1, width),
        linear_cotangent,
    )
    store = pl.pallas_call(
        store_all,
        out_shape=[jax.ShapeDtypeStruct((length, width), BF16)] * 8,
        in_specs=[anywhere] * 8,
        out_specs=[anywhere] * 8,
        scratch_shapes=[
            pltpu.VMEM((8, length, width), BF16),
            pltpu.SemaphoreType.DMA((8,)),
            pltpu.SemaphoreType.DMA((8,)),
        ],
        compiler_params=pltpu.CompilerParams(vmem_limit_bytes=60 * 1024 * 1024),
    )
    return tuple(store(*results))


def solution(mesh):
    tokens = P("ctx", "head")
    return jax.shard_map(
        body,
        mesh=mesh,
        in_specs=(
            tokens,
            tokens,
            tokens,
            P("ctx"),
            P("ctx", None),
            tokens,
            tokens,
            P("head", "ctx"),
            P("head"),
            tokens,
        ),
        out_specs=(tokens,) * 8,
        check_vma=False,
    )
```

```python
import functools
import math

import jax
import jax.numpy as jnp
from jax import lax
from jax.experimental import pallas as pl
from jax.experimental.pallas import tpu as pltpu
from jax.sharding import PartitionSpec as P

HD = 128
BLK = 128
REACH = 3
GROUP = 4
TAIL = 16
NEG = -1e30
EPSILON = 1e-05
MESH = pl.DeviceIdType.MESH
F32 = jnp.float32
BF16 = jnp.bfloat16


def dot(a, b, contract, precision=None):
    return lax.dot_general(
        a, b, (contract, ((), ())), precision=precision, preferred_element_type=F32
    )


def nn(a, b):
    return dot(a, b, ((1,), (0,)))


def nt(a, b):
    return dot(a, b, ((1,), (1,)))


def tn(a, b):
    return dot(a, b, ((0,), (0,)))


def kernel(
    n,
    groups,
    q_hbm,
    k_hbm,
    v_hbm,
    doc_hbm,
    list_hbm,
    lk_hbm,
    lv_hbm,
    decay_hbm,
    gain_hbm,
    cot_hbm,
    out_hbm,
    dq_hbm,
    dk_hbm,
    dv_hbm,
    lout_hbm,
    lqg_hbm,
    lkg_hbm,
    lvg_hbm,
    stage,
    leaving,
    doc_ref,
    list_ref,
    lk_ref,
    lv_ref,
    decay_ref,
    gain_ref,
    cot_ref,
    load,
    kbuf,
    vbuf,
    qbuf,
    gbuf,
    info,
    info_left,
    info_right,
    side,
    sidebuf,
    logs_out,
    logsbuf,
    score,
    up_send,
    up_recv,
    state_send,
    state_recv,
    back_send,
    back_recv,
    later_send,
    later_recv,
    sums,
    sums_recv,
    relayed,
    relay_send,
    relay_recv,
    near_send,
    near_recv,
    total_send,
    total_recv,
    total_sent,
    total_got,
    plane_send,
    plane_recv,
    head_send,
    head_recv,
):
    out_ref, dq_ref, dk_ref, dv_ref, lout_ref, lqg_ref, lkg_ref, lvg_ref = [
        stage.at[i] for i in range(8)
    ]
    homes = (out_hbm, dq_hbm, dk_hbm, dv_hbm, lout_hbm, lqg_hbm, lkg_hbm, lvg_hbm)
    leaves = [
        pltpu.make_async_copy(stage.at[i], homes[i], leaving.at[i]) for i in range(8)
    ]
    q_ref, k_ref, v_ref = qbuf.at[0], kbuf.at[0], vbuf.at[0]
    loads = [
        pltpu.make_async_copy(src, dst, load.at[i])
        for i, (src, dst) in enumerate(
            [
                (k_hbm, k_ref),
                (v_hbm, v_ref),
                (q_hbm, q_ref),
                (decay_hbm, decay_ref),
                (lk_hbm, lk_ref),
                (lv_hbm, lv_ref),
                (doc_hbm, doc_ref),
                (list_hbm, list_ref),
                (gain_hbm, gain_ref),
                (cot_hbm, cot_ref),
            ]
        )
    ]
    for copy in loads:
        copy.start()
    me = lax.axis_index("ctx")
    group = lax.axis_index("head")
    heads = q_hbm.shape[1] // HD
    scaling = 1.0 / math.sqrt(HD)
    cols = [slice(h * HD, (h + 1) * HD) for h in range(heads)]

    ext_at = lax.broadcasted_iota(jnp.int32, (TAIL, HD), 0)

    barrier = pltpu.get_barrier_semaphore()

    def greet(o, c):
        pl.semaphore_signal(
            barrier, inc=1, device_id={"ctx": lax.rem(me + o, n)}, device_id_type=MESH
        )
        return c

    lax.fori_loop(1, n, greet, 0)
    for o in range(1, groups):
        pl.semaphore_signal(
            barrier, inc=1, device_id={"head": lax.rem(group + o, groups)}, device_id_type=MESH
        )

    place = lax.rem(me, GROUP)
    plane = me // GROUP
    planes = n // GROUP

    def spread(lane, src, dst):
        for o in range(1, GROUP):
            j = lax.rem(place + o, GROUP)
            pltpu.make_async_remote_copy(
                src_ref=src.at[j],
                dst_ref=dst.at[place],
                send_sem=plane_send.at[lane, j],
                recv_sem=plane_recv.at[lane, place],
                device_id={"ctx": me - place + j},
                device_id_type=MESH,
            ).start()
        dst[place] = src[place]

    def collect(lane, src, dst):
        for o in range(1, GROUP):
            j = lax.rem(place + GROUP - o, GROUP)
            pltpu.make_async_remote_copy(
                src_ref=src.at[j],
                dst_ref=dst.at[j],
                send_sem=plane_send.at[lane, j],
                recv_sem=plane_recv.at[lane, j],
                device_id={"ctx": me - place + j},
                device_id_type=MESH,
            ).wait()

    def total_to(lane, o, way):
        return pltpu.make_async_remote_copy(
            src_ref=total_send.at[lane],
            dst_ref=total_recv.at[lane, o],
            send_sem=total_sent.at[lane, o],
            recv_sem=total_got.at[lane, o],
            device_id={"ctx": lax.rem(me + way * GROUP * o + n, n)},
            device_id_type=MESH,
        )

    def within(target):
        return (target >= 0) & (target < planes)

    def send_totals(lane, way):
        for o in range(1, planes):

            @pl.when(within(plane + way * o))
            def _():
                total_to(lane, o, way).start()

    def wait_totals(lane, way):
        for o in range(1, planes):

            @pl.when(within(plane + way * o))
            def _():
                total_to(lane, o, way).wait_send()

            @pl.when(within(plane - way * o))
            def _():
                total_to(lane, o, way).wait_recv()

    def with_tail(value, factor):
        high = factor.astype(BF16).astype(F32)
        tail = jnp.where(ext_at < TAIL // 2, high, factor - high)
        return jnp.concatenate([value, tail], axis=0).astype(BF16)

    def tail_of(piece):
        tail = piece[HD:, :].astype(F32)
        return tail[0:1, :] + tail[TAIL // 2 : TAIL // 2 + 1, :]

    def scan_plane(terms, factors, order):
        state = jnp.zeros((HD, HD), F32)
        product = jnp.ones((1, HD), F32)
        starts = [None] * GROUP
        for p in order:
            starts[p] = (state, product)
            state = factors[p] * state + terms[p]
            product = factors[p] * product
        return starts, state, product

    def incoming(lane, count):
        def one(i, state):
            piece = total_recv[lane, count - i]
            return tail_of(piece) * state + piece[:HD, :].astype(F32)

        return lax.fori_loop(0, count, one, jnp.zeros((HD, HD), F32))

    def near(kind, d, src, dst, step):
        return pltpu.make_async_remote_copy(
            src_ref=src,
            dst_ref=dst.at[d],
            send_sem=near_send.at[kind, d],
            recv_sem=near_recv.at[kind, d],
            device_id={"ctx": lax.rem(me + step + n, n)},
            device_id_type=MESH,
        )

    def send_small(kind, src, dst, way):
        for d in range(1, REACH + 1):
            target = me + way * d

            @pl.when((target >= 0) & (target < n))
            def _():
                near(kind, d, src, dst, way * d).start()

    def wait_small(kind, src, dst, way):
        for d in range(1, REACH + 1):
            target = me + way * d
            source = me - way * d

            @pl.when((target >= 0) & (target < n))
            def _():
                near(kind, d, src, dst, way * d).wait_send()

            @pl.when((source >= 0) & (source < n))
            def _():
                near(kind, d, src, dst, way * d).wait_recv()

    def ahead(way):
        return place if way > 0 else GROUP - 1 - place

    def inside(way, groups_on):
        target = me + way * GROUP * groups_on
        return (ahead(way) >= 1) & (target >= 0) & (target < n)

    def relay(kind, src, way):
        return pltpu.make_async_remote_copy(
            src_ref=src,
            dst_ref=relayed.at[kind],
            send_sem=relay_send.at[kind],
            recv_sem=relay_recv.at[kind],
            device_id={"ctx": lax.rem(me + way * GROUP + n, n)},
            device_id_type=MESH,
        )

    def send_across(kind, src, way):
        @pl.when(inside(way, 1))
        def _():
            relay(kind, src, way).start()

    def send_direct(kind, src, dst, way):
        for d in range(1, REACH + 1):

            @pl.when(ahead(way) + d < GROUP)
            def _():
                near(kind, d, src, dst, way * d).start()

    def forward_on(kind, src, dst, way):
        @pl.when(inside(way, -1))
        def _():
            relay(kind, src, way).wait_recv()
            for e in range(1, GROUP):

                @pl.when(e <= ahead(way))
                def _():
                    near(kind, GROUP - e, relayed.at[kind], dst, -way * e).start()

    def wait_block(kind, src, dst, way):
        for d in range(1, REACH + 1):
            source = me - way * d

            @pl.when((source >= 0) & (source < n))
            def _():
                near(kind, d, src, dst, way * d).wait_recv()

    def wait_sent(kind, src, dst, way):
        @pl.when(inside(way, 1))
        def _():
            relay(kind, src, way).wait_send()

        for d in range(1, REACH + 1):

            @pl.when(ahead(way) + d < GROUP)
            def _():
                near(kind, d, src, dst, way * d).wait_send()

        @pl.when(inside(way, -1))
        def _():
            for e in range(1, GROUP):

                @pl.when(e <= ahead(way))
                def _():
                    near(kind, GROUP - e, relayed.at[kind], dst, -way * e).wait_send()

    loads[0].wait()
    loads[1].wait()
    pl.semaphore_wait(barrier, n - 1 + groups - 1)
    send_across(1, k_ref, 1)
    send_direct(1, k_ref, kbuf, 1)
    send_across(2, v_ref, 1)
    send_direct(2, v_ref, vbuf, 1)
    loads[2].wait()
    send_across(4, q_ref, -1)

    loads[3].wait()
    row_at = lax.broadcasted_iota(jnp.int32, (BLK, BLK), 0)
    col_at = lax.broadcasted_iota(jnp.int32, (BLK, BLK), 1)
    lower = (row_at >= col_at).astype(F32)
    rates = decay_ref[...]
    exact = lax.Precision.HIGHEST
    run_col = dot(lower, rates, ((1,), (1,)), exact)
    run_row = dot(rates, lower, ((1,), (1,)), exact)
    last = dot(rates, jnp.ones((BLK, BLK), F32), ((1,), (0,)), exact)
    carry = jnp.exp(last)
    causal = row_at >= col_at

    at_col = [jnp.broadcast_to(run_col[:, h : h + 1], (BLK, HD)) for h in range(heads)]
    leave = [jnp.exp(last[h : h + 1, :] - at_col[h]) for h in range(heads)]
    enter = [jnp.exp(at_col[h]) for h in range(heads)]
    damping = [
        jnp.where(causal, jnp.exp(jnp.where(causal, at_col[h] - run_row[h : h + 1, :], 0.0)), 0.0)
        for h in range(heads)
    ]
    loads[4].wait()
    loads[5].wait()
    updates = [
        tn((lk_ref[:, cols[h]].astype(F32) * leave[h]).astype(BF16), lv_ref[:, cols[h]])
        for h in range(heads)
    ]
    for h in range(heads):
        up_send[h] = with_tail(updates[h], carry[h : h + 1, :])
    loads[6].wait()
    loads[7].wait()
    doc = jnp.full((1, HD), doc_ref[0].astype(F32))
    first = jnp.broadcast_to(list_ref[:, 0:1].astype(F32), (1, HD))
    second = jnp.broadcast_to(list_ref[:, 1:2].astype(F32), (1, HD))
    info_at = lax.broadcasted_iota(jnp.int32, (8, HD), 0)
    info[...] = jnp.where(info_at == 0, doc, jnp.where(info_at == 1, first, second))
    for d in range(1, REACH + 1):

        @pl.when(me - d < 0)
        def _():
            kbuf[d] = jnp.zeros_like(kbuf[d])
            vbuf[d] = jnp.zeros_like(vbuf[d])
            info_left[d] = jnp.full((8, HD), -1.0, F32)

        @pl.when(me + d >= n)
        def _():
            qbuf[d] = jnp.zeros_like(qbuf[d])
            gbuf[d] = jnp.zeros_like(gbuf[d])
            sidebuf[d] = jnp.zeros((2 * heads, HD), F32)
            logsbuf[d] = jnp.zeros((2 * heads, HD), F32)
            info_right[d] = jnp.full((8, HD), -1.0, F32)

    send_small(0, info, info_left, 1)
    send_small(3, info, info_right, -1)
    spread(0, up_send, up_recv)
    forward_on(1, k_ref, kbuf, 1)

    collect(0, up_send, up_recv)
    pieces = [up_recv[p] for p in range(GROUP)]
    factors = [tail_of(piece) for piece in pieces]
    terms = [piece[:HD, :].astype(F32) for piece in pieces]
    starts, state, product = scan_plane(terms, factors, range(GROUP))
    total_send[0] = with_tail(state, product)
    send_totals(0, 1)
    forward_on(2, v_ref, vbuf, 1)
    wait_totals(0, 1)
    state = incoming(0, plane)
    for p in range(GROUP):
        state_send[p] = (starts[p][1] * state + starts[p][0]).astype(BF16)
    spread(1, state_send, state_recv)

    wait_small(0, info, info_left, 1)
    wait_block(1, k_ref, kbuf, 1)
    bias = [jnp.where(causal, 0.0, NEG)]
    for d in range(1, REACH + 1):
        listed = (first == d - 1.0) | (second == d - 1.0)
        seen = (info_left[d][0:1, :] == doc) & listed
        bias.append(jnp.broadcast_to(jnp.where(seen, 0.0, NEG), (BLK, HD)))
    bias = jnp.concatenate(bias, axis=1)
    weights = []
    logsum = []
    for h in range(heads):
        keys = kbuf[:, :, cols[h]].reshape(-1, HD)
        s = nt(q_ref[:, cols[h]], keys) * scaling + bias
        score[h] = s
        m = jnp.max(s, axis=1, keepdims=True)
        e = jnp.exp(s - m)
        total = jnp.sum(e, axis=1, keepdims=True)
        weights.append((e * (1.0 / total)).astype(BF16))
        logsum.append(m + jnp.log(total))
    block = jnp.zeros((BLK, HD), F32)
    for h in range(heads):
        block = jnp.where(col_at == h, logsum[h], block)
    logs_out[...] = block.T[0 : 2 * heads, :]
    logsbuf[0] = logs_out[...]
    send_small(7, logs_out, logsbuf, -1)
    wait_block(2, v_ref, vbuf, 1)
    send_direct(4, q_ref, qbuf, -1)
    forward_on(4, q_ref, qbuf, -1)
    loads[8].wait()
    loads[9].wait()
    outs = []
    for h in range(heads):
        o = nn(weights[h], vbuf[:, :, cols[h]].reshape(-1, HD)).astype(BF16)
        outs.append(o)
        out_ref[:, cols[h]] = o
    leaves[0].start()

    mixing = [
        (nt(outs[h], lk_ref[:, cols[h]]) * damping[h]).astype(BF16) for h in range(heads)
    ]
    inner = [nn(mixing[h], lv_ref[:, cols[h]]) for h in range(heads)]
    collect(1, state_send, state_recv)
    states = state_recv[...].reshape(heads * HD, HD)
    raws = []
    scaled = []
    squares = jnp.zeros((BLK, HD), F32)
    cross = jnp.zeros((BLK, HD), F32)
    for h in range(heads):
        raw = inner[h] + enter[h] * nn(outs[h], states[h * HD : (h + 1) * HD])
        sc = cot_ref[:, cols[h]].astype(F32) * gain_ref[:, cols[h]]
        squares += raw * raw
        cross += sc * raw
        raws.append(raw)
        scaled.append(sc)
    sums[...] = jnp.where(
        col_at < HD // 2,
        jnp.sum(squares, axis=1, keepdims=True),
        jnp.sum(cross, axis=1, keepdims=True),
    )

    def to_head(o):
        return pltpu.make_async_remote_copy(
            src_ref=sums,
            dst_ref=sums_recv.at[o],
            send_sem=head_send.at[o],
            recv_sem=head_recv.at[o],
            device_id={"head": lax.rem(group + o, groups)},
            device_id_type=MESH,
        )

    for o in range(1, groups):
        to_head(o).start()
    qscaled = [(outs[h].astype(F32) * enter[h]).astype(BF16) for h in range(heads)]
    total = sums[...]
    for o in range(1, groups):
        to_head(o).wait()
        total = total + sums_recv[o]
    features = heads * HD * groups
    mean = jnp.broadcast_to(total[:, 0:1], (BLK, HD)) / features + EPSILON
    inverse = lax.rsqrt(mean)
    factor = jnp.broadcast_to(total[:, HD // 2 : HD // 2 + 1], (BLK, HD)) / (features * mean)
    halves = [((scaled[h] - raws[h] * factor) * inverse).astype(BF16) for h in range(heads)]
    mix_grads = []
    deltas = []
    gs = []
    for h in range(heads):
        mg = (nt(halves[h], lv_ref[:, cols[h]]) * damping[h]).astype(BF16)
        mix_grads.append(mg)
        g = nn(mg, lk_ref[:, cols[h]]) + enter[h] * nt(halves[h], states[h * HD : (h + 1) * HD])
        g = g.astype(BF16)
        lqg_ref[:, cols[h]] = g
        gbuf[0, :, cols[h]] = g
        gs.append(g)
    send_across(5, gbuf.at[0], -1)
    send_direct(5, gbuf.at[0], gbuf, -1)
    for h in range(heads):
        g = gs[h]
        deltas.append(
            jnp.sum(g.astype(F32) * outs[h].astype(F32), axis=1, keepdims=True)
        )
    block = jnp.zeros((BLK, HD), F32)
    for h in range(heads):
        block = jnp.where(col_at == h, deltas[h], block)
    side[...] = block.T[0 : 2 * heads, :]
    sidebuf[0] = side[...]
    send_small(6, side, sidebuf, -1)
    for h in range(heads):
        back = tn(qscaled[h], halves[h])
        back_send[h] = back.astype(BF16)
    spread(2, back_send, back_recv)

    leaves[5].start()
    for h in range(heads):
        lout_ref[:, cols[h]] = (raws[h] * inverse * gain_ref[:, cols[h]]).astype(BF16)
    leaves[4].start()
    for h in range(heads):
        chance = jnp.exp(score[h] - logsum[h])
        cg = nt(gbuf[0, :, cols[h]], vbuf[:, :, cols[h]].reshape(-1, HD))
        sg = (chance * (cg - deltas[h])).astype(BF16)
        keys = kbuf[:, :, cols[h]].reshape(-1, HD)
        dq_ref[:, cols[h]] = (nn(sg, keys) * scaling).astype(BF16)
    leaves[1].start()

    collect(2, back_send, back_recv)
    terms = [back_recv[p].astype(F32) for p in range(GROUP)]
    factors = [tail_of(up_recv[p]) for p in range(GROUP)]
    starts, state, product = scan_plane(terms, factors, range(GROUP - 1, -1, -1))
    total_send[1] = with_tail(state, product)
    send_totals(1, -1)
    key_local = [tn(mix_grads[h], outs[h]) for h in range(heads)]
    value_local = [tn(mixing[h], halves[h]) for h in range(heads)]
    forward_on(5, gbuf.at[0], gbuf, -1)
    wait_totals(1, -1)
    state = incoming(1, planes - 1 - plane)
    for p in range(GROUP):
        later_send[p] = (starts[p][1] * state + starts[p][0]).astype(BF16)
    spread(3, later_send, later_recv)

    wait_small(3, info, info_right, -1)
    wait_block(4, q_ref, qbuf, -1)
    bias = [jnp.where(row_at <= col_at, 0.0, NEG)]
    for d in range(1, REACH + 1):
        theirs = info_right[d]
        listed = (theirs[1:2, :] == d - 1.0) | (theirs[2:3, :] == d - 1.0)
        seen = (theirs[0:1, :] == doc) & listed
        bias.append(jnp.broadcast_to(jnp.where(seen, 0.0, NEG), (BLK, HD)))
    bias = jnp.concatenate(bias, axis=1)
    wait_small(7, logs_out, logsbuf, -1)
    for h in range(heads):
        queries = qbuf[:, :, cols[h]].reshape(-1, HD)
        logs = jnp.concatenate([logsbuf[d, h : h + 1, :] for d in range(REACH + 1)], axis=1)
        score[h] = jnp.exp(nt(k_ref[:, cols[h]], queries) * scaling + bias - logs)
    wait_block(5, gbuf.at[0], gbuf, -1)
    wait_small(6, side, sidebuf, -1)
    for h in range(heads):
        queries = qbuf[:, :, cols[h]].reshape(-1, HD)
        grads = gbuf[:, :, cols[h]].reshape(-1, HD)
        dels = jnp.concatenate(
            [sidebuf[d, h : h + 1, :] for d in range(REACH + 1)], axis=1
        )
        chance = score[h]
        dv_ref[:, cols[h]] = nn(chance.astype(BF16), grads).astype(BF16)
        cg = nt(v_ref[:, cols[h]], grads)
        sg = (chance * (cg - dels)).astype(BF16)
        dk_ref[:, cols[h]] = (nn(sg, queries) * scaling).astype(BF16)
    leaves[2].start()
    leaves[3].start()

    collect(3, later_send, later_recv)
    laters = later_recv[...].reshape(heads * HD, HD)
    for h in range(heads):
        later = laters[h * HD : (h + 1) * HD]
        lkg_ref[:, cols[h]] = (
            key_local[h] + leave[h] * nt(lv_ref[:, cols[h]], later)
        ).astype(BF16)
        lvg_ref[:, cols[h]] = (
            value_local[h] + leave[h] * nn(lk_ref[:, cols[h]], later)
        ).astype(BF16)
    leaves[6].start()
    leaves[7].start()
    wait_sent(1, k_ref, kbuf, 1)
    wait_sent(2, v_ref, vbuf, 1)
    wait_sent(4, q_ref, qbuf, -1)
    wait_sent(5, gbuf.at[0], gbuf, -1)
    for copy in leaves:
        copy.wait()


def store_all(*refs):
    held, arrived, done = refs[16:]
    loads = [pltpu.make_async_copy(refs[i], held.at[i], arrived.at[i]) for i in range(8)]
    stores = [pltpu.make_async_copy(held.at[i], refs[8 + i], done.at[i]) for i in range(8)]
    for load in loads:
        load.start()
    for load, store in zip(loads, stores):
        load.wait()
        store.start()
    for store in stores:
        store.wait()


def body(
    softmax_query,
    softmax_key,
    softmax_value,
    document_ids,
    block_lists,
    linear_key,
    linear_value,
    linear_decay,
    linear_gain,
    linear_cotangent,
):
    n = lax.axis_size("ctx")
    groups = lax.axis_size("head")
    length, width = softmax_query.shape
    heads = width // HD
    assert heads == GROUP and n % GROUP == 0
    anywhere = pl.BlockSpec(memory_space=pl.ANY)
    array = pltpu.VMEM((length, width), BF16)
    slots = REACH + 1
    window = pltpu.VMEM((slots, length, width), BF16)
    part = pltpu.VMEM((GROUP, HD, HD), BF16)
    results = pl.pallas_call(
        functools.partial(kernel, n, groups),
        out_shape=[jax.ShapeDtypeStruct((length, width), BF16)] * 8,
        in_specs=[anywhere] * 10,
        out_specs=[anywhere] * 8,
        scratch_shapes=[
            pltpu.VMEM((8, length, width), BF16),
            pltpu.SemaphoreType.DMA((8,)),
            pltpu.SMEM((1,), jnp.int32),
            pltpu.VMEM((1, 2), jnp.int32),
            array,
            array,
            pltpu.VMEM((heads, length), F32),
            pltpu.VMEM((1, width), F32),
            array,
            pltpu.SemaphoreType.DMA((10,)),
            window,
            window,
            window,
            window,
            pltpu.VMEM((8, HD), F32),
            pltpu.VMEM((slots, 8, HD), F32),
            pltpu.VMEM((slots, 8, HD), F32),
            pltpu.VMEM((2 * heads, HD), F32),
            pltpu.VMEM((slots, 2 * heads, HD), F32),
            pltpu.VMEM((2 * heads, HD), F32),
            pltpu.VMEM((slots, 2 * heads, HD), F32),
            pltpu.VMEM((heads, length, slots * HD), F32),
            pltpu.VMEM((GROUP, HD + TAIL, HD), BF16),
            pltpu.VMEM((GROUP, HD + TAIL, HD), BF16),
            part,
            part,
            part,
            part,
            part,
            part,
            pltpu.VMEM((length, HD), F32),
            pltpu.VMEM((groups, length, HD), F32),
            pltpu.VMEM((6, length, width), BF16),
            pltpu.SemaphoreType.DMA((6,)),
            pltpu.SemaphoreType.DMA((6,)),
            pltpu.SemaphoreType.DMA((8, slots)),
            pltpu.SemaphoreType.DMA((8, slots)),
            pltpu.VMEM((2, HD + TAIL, HD), BF16),
            pltpu.VMEM((2, n // GROUP, HD + TAIL, HD), BF16),
            pltpu.SemaphoreType.DMA((2, n // GROUP)),
            pltpu.SemaphoreType.DMA((2, n // GROUP)),
            pltpu.SemaphoreType.DMA((4, GROUP)),
            pltpu.SemaphoreType.DMA((4, GROUP)),
            pltpu.SemaphoreType.DMA((groups,)),
            pltpu.SemaphoreType.DMA((groups,)),
        ],
        compiler_params=pltpu.CompilerParams(
            collective_id=0, has_side_effects=True, vmem_limit_bytes=60 * 1024 * 1024
        ),
    )(
        softmax_query,
        softmax_key,
        softmax_value,
        document_ids,
        block_lists,
        linear_key,
        linear_value,
        linear_decay,
        linear_gain.reshape(1, width),
        linear_cotangent,
    )
    store = pl.pallas_call(
        store_all,
        out_shape=[jax.ShapeDtypeStruct((length, width), BF16)] * 8,
        in_specs=[anywhere] * 8,
        out_specs=[anywhere] * 8,
        scratch_shapes=[
            pltpu.VMEM((8, length, width), BF16),
            pltpu.SemaphoreType.DMA((8,)),
            pltpu.SemaphoreType.DMA((8,)),
        ],
        compiler_params=pltpu.CompilerParams(vmem_limit_bytes=60 * 1024 * 1024),
    )
    return tuple(store(*results))


def solution(mesh):
    tokens = P("ctx", "head")
    return jax.shard_map(
        body,
        mesh=mesh,
        in_specs=(
            tokens,
            tokens,
            tokens,
            P("ctx"),
            P("ctx", None),
            tokens,
            tokens,
            P("head", "ctx"),
            P("head"),
            tokens,
        ),
        out_specs=(tokens,) * 8,
        check_vma=False,
    )
```

```python
import functools
import math

import jax
import jax.numpy as jnp
from jax import lax
from jax.experimental import pallas as pl
from jax.experimental.pallas import tpu as pltpu
from jax.sharding import PartitionSpec as P

HD = 128
BLK = 128
REACH = 3
GROUP = 4
TAIL = 16
NEG = -1e30
EPSILON = 1e-05
MESH = pl.DeviceIdType.MESH
F32 = jnp.float32
BF16 = jnp.bfloat16


def dot(a, b, contract, precision=None):
    return lax.dot_general(
        a, b, (contract, ((), ())), precision=precision, preferred_element_type=F32
    )


def nn(a, b):
    return dot(a, b, ((1,), (0,)))


def nt(a, b):
    return dot(a, b, ((1,), (1,)))


def tn(a, b):
    return dot(a, b, ((0,), (0,)))


def kernel(
    n,
    groups,
    q_hbm,
    k_hbm,
    v_hbm,
    doc_hbm,
    list_hbm,
    lk_hbm,
    lv_hbm,
    decay_hbm,
    gain_hbm,
    cot_hbm,
    out_hbm,
    dq_hbm,
    dk_hbm,
    dv_hbm,
    lout_hbm,
    lqg_hbm,
    lkg_hbm,
    lvg_hbm,
    stage,
    leaving,
    doc_ref,
    list_ref,
    lk_ref,
    lv_ref,
    decay_ref,
    gain_ref,
    cot_ref,
    load,
    kbuf,
    vbuf,
    qbuf,
    gbuf,
    info,
    info_left,
    info_right,
    side,
    sidebuf,
    logs_out,
    logsbuf,
    score,
    up_send,
    up_recv,
    state_send,
    state_recv,
    back_send,
    back_recv,
    later_send,
    later_recv,
    sums,
    sums_recv,
    relayed,
    relay_send,
    relay_recv,
    near_send,
    near_recv,
    total_send,
    total_recv,
    total_sent,
    total_got,
    plane_send,
    plane_recv,
    head_send,
    head_recv,
):
    out_ref, dq_ref, dk_ref, dv_ref, lout_ref, lqg_ref, lkg_ref, lvg_ref = [
        stage.at[i] for i in range(8)
    ]
    homes = (out_hbm, dq_hbm, dk_hbm, dv_hbm, lout_hbm, lqg_hbm, lkg_hbm, lvg_hbm)
    leaves = [
        pltpu.make_async_copy(stage.at[i], homes[i], leaving.at[i]) for i in range(8)
    ]
    q_ref, k_ref, v_ref = qbuf.at[0], kbuf.at[0], vbuf.at[0]
    loads = [
        pltpu.make_async_copy(src, dst, load.at[i])
        for i, (src, dst) in enumerate(
            [
                (k_hbm, k_ref),
                (v_hbm, v_ref),
                (q_hbm, q_ref),
                (decay_hbm, decay_ref),
                (lk_hbm, lk_ref),
                (lv_hbm, lv_ref),
                (doc_hbm, doc_ref),
                (list_hbm, list_ref),
                (gain_hbm, gain_ref),
                (cot_hbm, cot_ref),
            ]
        )
    ]
    for copy in loads:
        copy.start()
    me = lax.axis_index("ctx")
    group = lax.axis_index("head")
    heads = q_hbm.shape[1] // HD
    scaling = 1.0 / math.sqrt(HD)
    cols = [slice(h * HD, (h + 1) * HD) for h in range(heads)]

    ext_at = lax.broadcasted_iota(jnp.int32, (TAIL, HD), 0)

    barrier = pltpu.get_barrier_semaphore()

    def greet(o, c):
        pl.semaphore_signal(
            barrier, inc=1, device_id={"ctx": lax.rem(me + o, n)}, device_id_type=MESH
        )
        return c

    lax.fori_loop(1, n, greet, 0)
    for o in range(1, groups):
        pl.semaphore_signal(
            barrier, inc=1, device_id={"head": lax.rem(group + o, groups)}, device_id_type=MESH
        )

    place = lax.rem(me, GROUP)
    plane = me // GROUP
    planes = n // GROUP

    def spread(lane, src, dst):
        for o in range(1, GROUP):
            j = lax.rem(place + o, GROUP)
            pltpu.make_async_remote_copy(
                src_ref=src.at[j],
                dst_ref=dst.at[place],
                send_sem=plane_send.at[lane, j],
                recv_sem=plane_recv.at[lane, place],
                device_id={"ctx": me - place + j},
                device_id_type=MESH,
            ).start()
        dst[place] = src[place]

    def collect(lane, src, dst):
        for o in range(1, GROUP):
            j = lax.rem(place + GROUP - o, GROUP)
            pltpu.make_async_remote_copy(
                src_ref=src.at[j],
                dst_ref=dst.at[j],
                send_sem=plane_send.at[lane, j],
                recv_sem=plane_recv.at[lane, j],
                device_id={"ctx": me - place + j},
                device_id_type=MESH,
            ).wait()

    def total_to(lane, o, way):
        return pltpu.make_async_remote_copy(
            src_ref=total_send.at[lane],
            dst_ref=total_recv.at[lane, o],
            send_sem=total_sent.at[lane, o],
            recv_sem=total_got.at[lane, o],
            device_id={"ctx": lax.rem(me + way * GROUP * o + n, n)},
            device_id_type=MESH,
        )

    def within(target):
        return (target >= 0) & (target < planes)

    def send_totals(lane, way):
        for o in range(1, planes):

            @pl.when(within(plane + way * o))
            def _():
                total_to(lane, o, way).start()

    def wait_totals(lane, way):
        for o in range(1, planes):

            @pl.when(within(plane + way * o))
            def _():
                total_to(lane, o, way).wait_send()

            @pl.when(within(plane - way * o))
            def _():
                total_to(lane, o, way).wait_recv()

    def with_tail(value, factor):
        high = factor.astype(BF16).astype(F32)
        tail = jnp.where(ext_at < TAIL // 2, high, factor - high)
        return jnp.concatenate([value, tail], axis=0).astype(BF16)

    def tail_of(piece):
        tail = piece[HD:, :].astype(F32)
        return tail[0:1, :] + tail[TAIL // 2 : TAIL // 2 + 1, :]

    def scan_plane(terms, factors, order):
        state = jnp.zeros((HD, HD), F32)
        product = jnp.ones((1, HD), F32)
        starts = [None] * GROUP
        for p in order:
            starts[p] = (state, product)
            state = factors[p] * state + terms[p]
            product = factors[p] * product
        return starts, state, product

    def incoming(lane, count):
        def one(i, state):
            piece = total_recv[lane, count - i]
            return tail_of(piece) * state + piece[:HD, :].astype(F32)

        return lax.fori_loop(0, count, one, jnp.zeros((HD, HD), F32))

    def near(kind, d, src, dst, step):
        return pltpu.make_async_remote_copy(
            src_ref=src,
            dst_ref=dst.at[d],
            send_sem=near_send.at[kind, d],
            recv_sem=near_recv.at[kind, d],
            device_id={"ctx": lax.rem(me + step + n, n)},
            device_id_type=MESH,
        )

    def send_small(kind, src, dst, way):
        for d in range(1, REACH + 1):
            target = me + way * d

            @pl.when((target >= 0) & (target < n))
            def _():
                near(kind, d, src, dst, way * d).start()

    def wait_small(kind, src, dst, way):
        for d in range(1, REACH + 1):
            target = me + way * d
            source = me - way * d

            @pl.when((target >= 0) & (target < n))
            def _():
                near(kind, d, src, dst, way * d).wait_send()

            @pl.when((source >= 0) & (source < n))
            def _():
                near(kind, d, src, dst, way * d).wait_recv()

    def ahead(way):
        return place if way > 0 else GROUP - 1 - place

    def inside(way, groups_on):
        target = me + way * GROUP * groups_on
        return (ahead(way) >= 1) & (target >= 0) & (target < n)

    def relay(kind, src, way):
        return pltpu.make_async_remote_copy(
            src_ref=src,
            dst_ref=relayed.at[kind],
            send_sem=relay_send.at[kind],
            recv_sem=relay_recv.at[kind],
            device_id={"ctx": lax.rem(me + way * GROUP + n, n)},
            device_id_type=MESH,
        )

    def send_across(kind, src, way):
        @pl.when(inside(way, 1))
        def _():
            relay(kind, src, way).start()

    def send_direct(kind, src, dst, way):
        for d in range(1, REACH + 1):

            @pl.when(ahead(way) + d < GROUP)
            def _():
                near(kind, d, src, dst, way * d).start()

    def forward_on(kind, src, dst, way):
        @pl.when(inside(way, -1))
        def _():
            relay(kind, src, way).wait_recv()
            for e in range(1, GROUP):

                @pl.when(e <= ahead(way))
                def _():
                    near(kind, GROUP - e, relayed.at[kind], dst, -way * e).start()

    def wait_block(kind, src, dst, way):
        for d in range(1, REACH + 1):
            source = me - way * d

            @pl.when((source >= 0) & (source < n))
            def _():
                near(kind, d, src, dst, way * d).wait_recv()

    def wait_sent(kind, src, dst, way):
        @pl.when(inside(way, 1))
        def _():
            relay(kind, src, way).wait_send()

        for d in range(1, REACH + 1):

            @pl.when(ahead(way) + d < GROUP)
            def _():
                near(kind, d, src, dst, way * d).wait_send()

        @pl.when(inside(way, -1))
        def _():
            for e in range(1, GROUP):

                @pl.when(e <= ahead(way))
                def _():
                    near(kind, GROUP - e, relayed.at[kind], dst, -way * e).wait_send()

    loads[3].wait()
    row_at = lax.broadcasted_iota(jnp.int32, (BLK, BLK), 0)
    col_at = lax.broadcasted_iota(jnp.int32, (BLK, BLK), 1)
    lower = (row_at >= col_at).astype(F32)
    rates = decay_ref[...]
    exact = lax.Precision.HIGHEST
    run_col = dot(lower, rates, ((1,), (1,)), exact)
    last = dot(rates, jnp.ones((BLK, BLK), F32), ((1,), (0,)), exact)
    carry = jnp.exp(last)
    causal = row_at >= col_at

    at_col = [jnp.broadcast_to(run_col[:, h : h + 1], (BLK, HD)) for h in range(heads)]
    leave = [jnp.exp(last[h : h + 1, :] - at_col[h]) for h in range(heads)]
    loads[4].wait()
    loads[5].wait()
    updates = [
        tn((lk_ref[:, cols[h]].astype(F32) * leave[h]).astype(BF16), lv_ref[:, cols[h]])
        for h in range(heads)
    ]
    for h in range(heads):
        up_send[h] = with_tail(updates[h], carry[h : h + 1, :])
    loads[6].wait()
    loads[7].wait()
    doc = jnp.full((1, HD), doc_ref[0].astype(F32))
    first = jnp.broadcast_to(list_ref[:, 0:1].astype(F32), (1, HD))
    second = jnp.broadcast_to(list_ref[:, 1:2].astype(F32), (1, HD))
    info_at = lax.broadcasted_iota(jnp.int32, (8, HD), 0)
    info[...] = jnp.where(info_at == 0, doc, jnp.where(info_at == 1, first, second))
    pl.semaphore_wait(barrier, n - 1 + groups - 1)
    spread(0, up_send, up_recv)
    send_small(0, info, info_left, 1)
    loads[0].wait()
    loads[1].wait()
    send_across(1, k_ref, 1)
    send_direct(1, k_ref, kbuf, 1)
    send_across(2, v_ref, 1)
    send_direct(2, v_ref, vbuf, 1)
    loads[2].wait()
    send_across(4, q_ref, -1)
    run_row = dot(rates, lower, ((1,), (1,)), exact)
    enter = [jnp.exp(at_col[h]) for h in range(heads)]
    damping = [
        jnp.where(causal, jnp.exp(jnp.where(causal, at_col[h] - run_row[h : h + 1, :], 0.0)), 0.0)
        for h in range(heads)
    ]
    for d in range(1, REACH + 1):

        @pl.when(me - d < 0)
        def _():
            kbuf[d] = jnp.zeros_like(kbuf[d])
            vbuf[d] = jnp.zeros_like(vbuf[d])
            info_left[d] = jnp.full((8, HD), -1.0, F32)

        @pl.when(me + d >= n)
        def _():
            qbuf[d] = jnp.zeros_like(qbuf[d])
            gbuf[d] = jnp.zeros_like(gbuf[d])
            sidebuf[d] = jnp.zeros((2 * heads, HD), F32)
            logsbuf[d] = jnp.zeros((2 * heads, HD), F32)
            info_right[d] = jnp.full((8, HD), -1.0, F32)

    send_small(3, info, info_right, -1)
    forward_on(1, k_ref, kbuf, 1)

    collect(0, up_send, up_recv)
    pieces = [up_recv[p] for p in range(GROUP)]
    factors = [tail_of(piece) for piece in pieces]
    terms = [piece[:HD, :].astype(F32) for piece in pieces]
    starts, state, product = scan_plane(terms, factors, range(GROUP))
    total_send[0] = with_tail(state, product)
    send_totals(0, 1)
    forward_on(2, v_ref, vbuf, 1)
    wait_totals(0, 1)
    state = incoming(0, plane)
    for p in range(GROUP):
        state_send[p] = (starts[p][1] * state + starts[p][0]).astype(BF16)
    spread(1, state_send, state_recv)

    wait_small(0, info, info_left, 1)
    wait_block(1, k_ref, kbuf, 1)
    bias = [jnp.where(causal, 0.0, NEG)]
    for d in range(1, REACH + 1):
        listed = (first == d - 1.0) | (second == d - 1.0)
        seen = (info_left[d][0:1, :] == doc) & listed
        bias.append(jnp.broadcast_to(jnp.where(seen, 0.0, NEG), (BLK, HD)))
    bias = jnp.concatenate(bias, axis=1)
    weights = []
    logsum = []
    for h in range(heads):
        keys = kbuf[:, :, cols[h]].reshape(-1, HD)
        s = nt(q_ref[:, cols[h]], keys) * scaling + bias
        score[h] = s
        m = jnp.max(s, axis=1, keepdims=True)
        e = jnp.exp(s - m)
        total = jnp.sum(e, axis=1, keepdims=True)
        weights.append((e * (1.0 / total)).astype(BF16))
        logsum.append(m + jnp.log(total))
    block = jnp.zeros((BLK, HD), F32)
    for h in range(heads):
        block = jnp.where(col_at == h, logsum[h], block)
    logs_out[...] = block.T[0 : 2 * heads, :]
    logsbuf[0] = logs_out[...]
    send_small(7, logs_out, logsbuf, -1)
    wait_block(2, v_ref, vbuf, 1)
    send_direct(4, q_ref, qbuf, -1)
    forward_on(4, q_ref, qbuf, -1)
    loads[8].wait()
    loads[9].wait()
    outs = []
    for h in range(heads):
        o = nn(weights[h], vbuf[:, :, cols[h]].reshape(-1, HD)).astype(BF16)
        outs.append(o)
        out_ref[:, cols[h]] = o
    leaves[0].start()

    mixing = [
        (nt(outs[h], lk_ref[:, cols[h]]) * damping[h]).astype(BF16) for h in range(heads)
    ]
    inner = [nn(mixing[h], lv_ref[:, cols[h]]) for h in range(heads)]
    collect(1, state_send, state_recv)
    states = state_recv[...].reshape(heads * HD, HD)
    raws = []
    scaled = []
    squares = jnp.zeros((BLK, HD), F32)
    cross = jnp.zeros((BLK, HD), F32)
    for h in range(heads):
        raw = inner[h] + enter[h] * nn(outs[h], states[h * HD : (h + 1) * HD])
        sc = cot_ref[:, cols[h]].astype(F32) * gain_ref[:, cols[h]]
        squares += raw * raw
        cross += sc * raw
        raws.append(raw)
        scaled.append(sc)
    sums[...] = jnp.where(
        col_at < HD // 2,
        jnp.sum(squares, axis=1, keepdims=True),
        jnp.sum(cross, axis=1, keepdims=True),
    )

    def to_head(o):
        return pltpu.make_async_remote_copy(
            src_ref=sums,
            dst_ref=sums_recv.at[o],
            send_sem=head_send.at[o],
            recv_sem=head_recv.at[o],
            device_id={"head": lax.rem(group + o, groups)},
            device_id_type=MESH,
        )

    for o in range(1, groups):
        to_head(o).start()
    qscaled = [(outs[h].astype(F32) * enter[h]).astype(BF16) for h in range(heads)]
    total = sums[...]
    for o in range(1, groups):
        to_head(o).wait()
        total = total + sums_recv[o]
    features = heads * HD * groups
    mean = jnp.broadcast_to(total[:, 0:1], (BLK, HD)) / features + EPSILON
    inverse = lax.rsqrt(mean)
    factor = jnp.broadcast_to(total[:, HD // 2 : HD // 2 + 1], (BLK, HD)) / (features * mean)
    halves = [((scaled[h] - raws[h] * factor) * inverse).astype(BF16) for h in range(heads)]
    for h in range(heads):
        back = tn(qscaled[h], halves[h])
        back_send[h] = back.astype(BF16)
    spread(2, back_send, back_recv)
    mix_grads = []
    deltas = []
    gs = []
    for h in range(heads):
        mg = (nt(halves[h], lv_ref[:, cols[h]]) * damping[h]).astype(BF16)
        mix_grads.append(mg)
        g = nn(mg, lk_ref[:, cols[h]]) + enter[h] * nt(halves[h], states[h * HD : (h + 1) * HD])
        g = g.astype(BF16)
        lqg_ref[:, cols[h]] = g
        gbuf[0, :, cols[h]] = g
        gs.append(g)
    send_across(5, gbuf.at[0], -1)
    send_direct(5, gbuf.at[0], gbuf, -1)
    for h in range(heads):
        g = gs[h]
        deltas.append(
            jnp.sum(g.astype(F32) * outs[h].astype(F32), axis=1, keepdims=True)
        )
    block = jnp.zeros((BLK, HD), F32)
    for h in range(heads):
        block = jnp.where(col_at == h, deltas[h], block)
    side[...] = block.T[0 : 2 * heads, :]
    sidebuf[0] = side[...]
    send_small(6, side, sidebuf, -1)
    leaves[5].start()
    for h in range(heads):
        lout_ref[:, cols[h]] = (raws[h] * inverse * gain_ref[:, cols[h]]).astype(BF16)
    leaves[4].start()
    for h in range(heads):
        chance = jnp.exp(score[h] - logsum[h])
        cg = nt(gbuf[0, :, cols[h]], vbuf[:, :, cols[h]].reshape(-1, HD))
        sg = (chance * (cg - deltas[h])).astype(BF16)
        keys = kbuf[:, :, cols[h]].reshape(-1, HD)
        dq_ref[:, cols[h]] = (nn(sg, keys) * scaling).astype(BF16)
    leaves[1].start()

    collect(2, back_send, back_recv)
    terms = [back_recv[p].astype(F32) for p in range(GROUP)]
    factors = [tail_of(up_recv[p]) for p in range(GROUP)]
    starts, state, product = scan_plane(terms, factors, range(GROUP - 1, -1, -1))
    total_send[1] = with_tail(state, product)
    send_totals(1, -1)
    forward_on(5, gbuf.at[0], gbuf, -1)
    key_local = [tn(mix_grads[h], outs[h]) for h in range(heads)]
    value_local = [tn(mixing[h], halves[h]) for h in range(heads)]
    wait_totals(1, -1)
    state = incoming(1, planes - 1 - plane)
    for p in range(GROUP):
        later_send[p] = (starts[p][1] * state + starts[p][0]).astype(BF16)
    spread(3, later_send, later_recv)

    wait_small(3, info, info_right, -1)
    wait_block(4, q_ref, qbuf, -1)
    bias = [jnp.where(row_at <= col_at, 0.0, NEG)]
    for d in range(1, REACH + 1):
        theirs = info_right[d]
        listed = (theirs[1:2, :] == d - 1.0) | (theirs[2:3, :] == d - 1.0)
        seen = (theirs[0:1, :] == doc) & listed
        bias.append(jnp.broadcast_to(jnp.where(seen, 0.0, NEG), (BLK, HD)))
    bias = jnp.concatenate(bias, axis=1)
    wait_small(7, logs_out, logsbuf, -1)
    for h in range(heads):
        queries = qbuf[:, :, cols[h]].reshape(-1, HD)
        logs = jnp.concatenate([logsbuf[d, h : h + 1, :] for d in range(REACH + 1)], axis=1)
        score[h] = jnp.exp(nt(k_ref[:, cols[h]], queries) * scaling + bias - logs)
    wait_block(5, gbuf.at[0], gbuf, -1)
    wait_small(6, side, sidebuf, -1)
    for h in range(heads):
        queries = qbuf[:, :, cols[h]].reshape(-1, HD)
        grads = gbuf[:, :, cols[h]].reshape(-1, HD)
        dels = jnp.concatenate(
            [sidebuf[d, h : h + 1, :] for d in range(REACH + 1)], axis=1
        )
        chance = score[h]
        dv_ref[:, cols[h]] = nn(chance.astype(BF16), grads).astype(BF16)
        cg = nt(v_ref[:, cols[h]], grads)
        sg = (chance * (cg - dels)).astype(BF16)
        dk_ref[:, cols[h]] = (nn(sg, queries) * scaling).astype(BF16)
    leaves[2].start()
    leaves[3].start()

    collect(3, later_send, later_recv)
    laters = later_recv[...].reshape(heads * HD, HD)
    for h in range(heads):
        later = laters[h * HD : (h + 1) * HD]
        lkg_ref[:, cols[h]] = (
            key_local[h] + leave[h] * nt(lv_ref[:, cols[h]], later)
        ).astype(BF16)
        lvg_ref[:, cols[h]] = (
            value_local[h] + leave[h] * nn(lk_ref[:, cols[h]], later)
        ).astype(BF16)
    leaves[6].start()
    leaves[7].start()
    wait_sent(1, k_ref, kbuf, 1)
    wait_sent(2, v_ref, vbuf, 1)
    wait_sent(4, q_ref, qbuf, -1)
    wait_sent(5, gbuf.at[0], gbuf, -1)
    for copy in leaves:
        copy.wait()


def store_all(*refs):
    held, arrived, done = refs[16:]
    loads = [pltpu.make_async_copy(refs[i], held.at[i], arrived.at[i]) for i in range(8)]
    stores = [pltpu.make_async_copy(held.at[i], refs[8 + i], done.at[i]) for i in range(8)]
    for load in loads:
        load.start()
    for load, store in zip(loads, stores):
        load.wait()
        store.start()
    for store in stores:
        store.wait()


def body(
    softmax_query,
    softmax_key,
    softmax_value,
    document_ids,
    block_lists,
    linear_key,
    linear_value,
    linear_decay,
    linear_gain,
    linear_cotangent,
):
    n = lax.axis_size("ctx")
    groups = lax.axis_size("head")
    length, width = softmax_query.shape
    heads = width // HD
    assert heads == GROUP and n % GROUP == 0
    anywhere = pl.BlockSpec(memory_space=pl.ANY)
    array = pltpu.VMEM((length, width), BF16)
    slots = REACH + 1
    window = pltpu.VMEM((slots, length, width), BF16)
    part = pltpu.VMEM((GROUP, HD, HD), BF16)
    results = pl.pallas_call(
        functools.partial(kernel, n, groups),
        out_shape=[jax.ShapeDtypeStruct((length, width), BF16)] * 8,
        in_specs=[anywhere] * 10,
        out_specs=[anywhere] * 8,
        scratch_shapes=[
            pltpu.VMEM((8, length, width), BF16),
            pltpu.SemaphoreType.DMA((8,)),
            pltpu.SMEM((1,), jnp.int32),
            pltpu.VMEM((1, 2), jnp.int32),
            array,
            array,
            pltpu.VMEM((heads, length), F32),
            pltpu.VMEM((1, width), F32),
            array,
            pltpu.SemaphoreType.DMA((10,)),
            window,
            window,
            window,
            window,
            pltpu.VMEM((8, HD), F32),
            pltpu.VMEM((slots, 8, HD), F32),
            pltpu.VMEM((slots, 8, HD), F32),
            pltpu.VMEM((2 * heads, HD), F32),
            pltpu.VMEM((slots, 2 * heads, HD), F32),
            pltpu.VMEM((2 * heads, HD), F32),
            pltpu.VMEM((slots, 2 * heads, HD), F32),
            pltpu.VMEM((heads, length, slots * HD), F32),
            pltpu.VMEM((GROUP, HD + TAIL, HD), BF16),
            pltpu.VMEM((GROUP, HD + TAIL, HD), BF16),
            part,
            part,
            part,
            part,
            part,
            part,
            pltpu.VMEM((length, HD), F32),
            pltpu.VMEM((groups, length, HD), F32),
            pltpu.VMEM((6, length, width), BF16),
            pltpu.SemaphoreType.DMA((6,)),
            pltpu.SemaphoreType.DMA((6,)),
            pltpu.SemaphoreType.DMA((8, slots)),
            pltpu.SemaphoreType.DMA((8, slots)),
            pltpu.VMEM((2, HD + TAIL, HD), BF16),
            pltpu.VMEM((2, n // GROUP, HD + TAIL, HD), BF16),
            pltpu.SemaphoreType.DMA((2, n // GROUP)),
            pltpu.SemaphoreType.DMA((2, n // GROUP)),
            pltpu.SemaphoreType.DMA((4, GROUP)),
            pltpu.SemaphoreType.DMA((4, GROUP)),
            pltpu.SemaphoreType.DMA((groups,)),
            pltpu.SemaphoreType.DMA((groups,)),
        ],
        compiler_params=pltpu.CompilerParams(
            collective_id=0, has_side_effects=True, vmem_limit_bytes=60 * 1024 * 1024
        ),
    )(
        softmax_query,
        softmax_key,
        softmax_value,
        document_ids,
        block_lists,
        linear_key,
        linear_value,
        linear_decay,
        linear_gain.reshape(1, width),
        linear_cotangent,
    )
    store = pl.pallas_call(
        store_all,
        out_shape=[jax.ShapeDtypeStruct((length, width), BF16)] * 8,
        in_specs=[anywhere] * 8,
        out_specs=[anywhere] * 8,
        scratch_shapes=[
            pltpu.VMEM((8, length, width), BF16),
            pltpu.SemaphoreType.DMA((8,)),
            pltpu.SemaphoreType.DMA((8,)),
        ],
        compiler_params=pltpu.CompilerParams(vmem_limit_bytes=60 * 1024 * 1024),
    )
    return tuple(store(*results))


def solution(mesh):
    tokens = P("ctx", "head")
    return jax.shard_map(
        body,
        mesh=mesh,
        in_specs=(
            tokens,
            tokens,
            tokens,
            P("ctx"),
            P("ctx", None),
            tokens,
            tokens,
            P("head", "ctx"),
            P("head"),
            tokens,
        ),
        out_specs=(tokens,) * 8,
        check_vma=False,
    )
```

```python
import functools
import math

import jax
import jax.numpy as jnp
from jax import lax
from jax.experimental import pallas as pl
from jax.experimental.pallas import tpu as pltpu
from jax.sharding import PartitionSpec as P

HD = 128
BLK = 128
REACH = 3
GROUP = 4
TAIL = 16
NEG = -1e30
EPSILON = 1e-05
MESH = pl.DeviceIdType.MESH
F32 = jnp.float32
BF16 = jnp.bfloat16


def dot(a, b, contract, precision=None):
    return lax.dot_general(
        a, b, (contract, ((), ())), precision=precision, preferred_element_type=F32
    )


def nn(a, b):
    return dot(a, b, ((1,), (0,)))


def nt(a, b):
    return dot(a, b, ((1,), (1,)))


def tn(a, b):
    return dot(a, b, ((0,), (0,)))


def kernel(
    n,
    groups,
    q_hbm,
    k_hbm,
    v_hbm,
    doc_hbm,
    list_hbm,
    lk_hbm,
    lv_hbm,
    decay_hbm,
    gain_hbm,
    cot_hbm,
    out_hbm,
    dq_hbm,
    dk_hbm,
    dv_hbm,
    lout_hbm,
    lqg_hbm,
    lkg_hbm,
    lvg_hbm,
    stage,
    leaving,
    doc_ref,
    list_ref,
    lk_ref,
    lv_ref,
    decay_ref,
    gain_ref,
    cot_ref,
    load,
    kbuf,
    vbuf,
    qbuf,
    gbuf,
    info,
    info_left,
    info_right,
    side,
    sidebuf,
    logs_out,
    logsbuf,
    score,
    up_send,
    up_recv,
    state_send,
    state_recv,
    back_send,
    back_recv,
    later_send,
    later_recv,
    sums,
    sums_recv,
    relayed,
    relay_send,
    relay_recv,
    near_send,
    near_recv,
    total_send,
    total_recv,
    total_sent,
    total_got,
    plane_send,
    plane_recv,
    head_send,
    head_recv,
):
    out_ref, dq_ref, dk_ref, dv_ref, lout_ref, lqg_ref, lkg_ref, lvg_ref = [
        stage.at[i] for i in range(8)
    ]
    homes = (out_hbm, dq_hbm, dk_hbm, dv_hbm, lout_hbm, lqg_hbm, lkg_hbm, lvg_hbm)
    leaves = [
        pltpu.make_async_copy(stage.at[i], homes[i], leaving.at[i]) for i in range(8)
    ]
    q_ref, k_ref, v_ref = qbuf.at[0], kbuf.at[0], vbuf.at[0]
    loads = [
        pltpu.make_async_copy(src, dst, load.at[i])
        for i, (src, dst) in enumerate(
            [
                (k_hbm, k_ref),
                (v_hbm, v_ref),
                (q_hbm, q_ref),
                (decay_hbm, decay_ref),
                (lk_hbm, lk_ref),
                (lv_hbm, lv_ref),
                (doc_hbm, doc_ref),
                (list_hbm, list_ref),
                (gain_hbm, gain_ref),
                (cot_hbm, cot_ref),
            ]
        )
    ]
    for copy in loads:
        copy.start()
    me = lax.axis_index("ctx")
    group = lax.axis_index("head")
    heads = q_hbm.shape[1] // HD
    scaling = 1.0 / math.sqrt(HD)
    cols = [slice(h * HD, (h + 1) * HD) for h in range(heads)]

    ext_at = lax.broadcasted_iota(jnp.int32, (TAIL, HD), 0)

    barrier = pltpu.get_barrier_semaphore()

    def greet(o, c):
        pl.semaphore_signal(
            barrier, inc=1, device_id={"ctx": lax.rem(me + o, n)}, device_id_type=MESH
        )
        return c

    lax.fori_loop(1, n, greet, 0)
    for o in range(1, groups):
        pl.semaphore_signal(
            barrier, inc=1, device_id={"head": lax.rem(group + o, groups)}, device_id_type=MESH
        )

    place = lax.rem(me, GROUP)
    plane = me // GROUP
    planes = n // GROUP

    def spread(lane, src, dst):
        for o in range(1, GROUP):
            j = lax.rem(place + o, GROUP)
            pltpu.make_async_remote_copy(
                src_ref=src.at[j],
                dst_ref=dst.at[place],
                send_sem=plane_send.at[lane, j],
                recv_sem=plane_recv.at[lane, place],
                device_id={"ctx": me - place + j},
                device_id_type=MESH,
            ).start()
        dst[place] = src[place]

    def collect(lane, src, dst):
        for o in range(1, GROUP):
            j = lax.rem(place + GROUP - o, GROUP)
            pltpu.make_async_remote_copy(
                src_ref=src.at[j],
                dst_ref=dst.at[j],
                send_sem=plane_send.at[lane, j],
                recv_sem=plane_recv.at[lane, j],
                device_id={"ctx": me - place + j},
                device_id_type=MESH,
            ).wait()

    def total_to(lane, o, way):
        return pltpu.make_async_remote_copy(
            src_ref=total_send.at[lane],
            dst_ref=total_recv.at[lane, o],
            send_sem=total_sent.at[lane, o],
            recv_sem=total_got.at[lane, o],
            device_id={"ctx": lax.rem(me + way * GROUP * o + n, n)},
            device_id_type=MESH,
        )

    def within(target):
        return (target >= 0) & (target < planes)

    def send_totals(lane, way):
        for o in range(1, planes):

            @pl.when(within(plane + way * o))
            def _():
                total_to(lane, o, way).start()

    def wait_totals(lane, way):
        for o in range(1, planes):

            @pl.when(within(plane + way * o))
            def _():
                total_to(lane, o, way).wait_send()

            @pl.when(within(plane - way * o))
            def _():
                total_to(lane, o, way).wait_recv()

    def with_tail(value, factor):
        high = factor.astype(BF16).astype(F32)
        tail = jnp.where(ext_at < TAIL // 2, high, factor - high)
        return jnp.concatenate([value, tail], axis=0).astype(BF16)

    def tail_of(piece):
        tail = piece[HD:, :].astype(F32)
        return tail[0:1, :] + tail[TAIL // 2 : TAIL // 2 + 1, :]

    def scan_plane(terms, factors, order):
        state = jnp.zeros((HD, HD), F32)
        product = jnp.ones((1, HD), F32)
        starts = [None] * GROUP
        for p in order:
            starts[p] = (state, product)
            state = factors[p] * state + terms[p]
            product = factors[p] * product
        return starts, state, product

    def incoming(lane, count):
        def one(i, state):
            piece = total_recv[lane, count - i]
            return tail_of(piece) * state + piece[:HD, :].astype(F32)

        return lax.fori_loop(0, count, one, jnp.zeros((HD, HD), F32))

    def near(kind, d, src, dst, step):
        return pltpu.make_async_remote_copy(
            src_ref=src,
            dst_ref=dst.at[d],
            send_sem=near_send.at[kind, d],
            recv_sem=near_recv.at[kind, d],
            device_id={"ctx": lax.rem(me + step + n, n)},
            device_id_type=MESH,
        )

    def send_small(kind, src, dst, way):
        for d in range(1, REACH + 1):
            target = me + way * d

            @pl.when((target >= 0) & (target < n))
            def _():
                near(kind, d, src, dst, way * d).start()

    def wait_small(kind, src, dst, way):
        for d in range(1, REACH + 1):
            target = me + way * d
            source = me - way * d

            @pl.when((target >= 0) & (target < n))
            def _():
                near(kind, d, src, dst, way * d).wait_send()

            @pl.when((source >= 0) & (source < n))
            def _():
                near(kind, d, src, dst, way * d).wait_recv()

    def ahead(way):
        return place if way > 0 else GROUP - 1 - place

    def inside(way, groups_on):
        target = me + way * GROUP * groups_on
        return (ahead(way) >= 1) & (target >= 0) & (target < n)

    def relay(kind, src, way):
        return pltpu.make_async_remote_copy(
            src_ref=src,
            dst_ref=relayed.at[kind],
            send_sem=relay_send.at[kind],
            recv_sem=relay_recv.at[kind],
            device_id={"ctx": lax.rem(me + way * GROUP + n, n)},
            device_id_type=MESH,
        )

    def send_across(kind, src, way):
        @pl.when(inside(way, 1))
        def _():
            relay(kind, src, way).start()

    def send_direct(kind, src, dst, way):
        for d in range(1, REACH + 1):

            @pl.when(ahead(way) + d < GROUP)
            def _():
                near(kind, d, src, dst, way * d).start()

    def forward_on(kind, src, dst, way):
        @pl.when(inside(way, -1))
        def _():
            relay(kind, src, way).wait_recv()
            for e in range(1, GROUP):

                @pl.when(e <= ahead(way))
                def _():
                    near(kind, GROUP - e, relayed.at[kind], dst, -way * e).start()

    def wait_block(kind, src, dst, way):
        for d in range(1, REACH + 1):
            source = me - way * d

            @pl.when((source >= 0) & (source < n))
            def _():
                near(kind, d, src, dst, way * d).wait_recv()

    def wait_sent(kind, src, dst, way):
        @pl.when(inside(way, 1))
        def _():
            relay(kind, src, way).wait_send()

        for d in range(1, REACH + 1):

            @pl.when(ahead(way) + d < GROUP)
            def _():
                near(kind, d, src, dst, way * d).wait_send()

        @pl.when(inside(way, -1))
        def _():
            for e in range(1, GROUP):

                @pl.when(e <= ahead(way))
                def _():
                    near(kind, GROUP - e, relayed.at[kind], dst, -way * e).wait_send()

    loads[3].wait()
    row_at = lax.broadcasted_iota(jnp.int32, (BLK, BLK), 0)
    col_at = lax.broadcasted_iota(jnp.int32, (BLK, BLK), 1)
    lower = (row_at >= col_at).astype(F32)
    rates = decay_ref[...]
    exact = lax.Precision.HIGHEST
    run_col = dot(lower, rates, ((1,), (1,)), exact)
    last = dot(rates, jnp.ones((BLK, BLK), F32), ((1,), (0,)), exact)
    carry = jnp.exp(last)
    causal = row_at >= col_at

    at_col = [jnp.broadcast_to(run_col[:, h : h + 1], (BLK, HD)) for h in range(heads)]
    leave = [jnp.exp(last[h : h + 1, :] - at_col[h]) for h in range(heads)]
    loads[4].wait()
    loads[5].wait()
    updates = [
        tn((lk_ref[:, cols[h]].astype(F32) * leave[h]).astype(BF16), lv_ref[:, cols[h]])
        for h in range(heads)
    ]
    for h in range(heads):
        up_send[h] = with_tail(updates[h], carry[h : h + 1, :])
    loads[6].wait()
    loads[7].wait()
    doc = jnp.full((1, HD), doc_ref[0].astype(F32))
    first = jnp.broadcast_to(list_ref[:, 0:1].astype(F32), (1, HD))
    second = jnp.broadcast_to(list_ref[:, 1:2].astype(F32), (1, HD))
    info_at = lax.broadcasted_iota(jnp.int32, (8, HD), 0)
    info[...] = jnp.where(info_at == 0, doc, jnp.where(info_at == 1, first, second))
    pl.semaphore_wait(barrier, n - 1 + groups - 1)
    spread(0, up_send, up_recv)
    send_small(0, info, info_left, 1)
    loads[0].wait()
    loads[1].wait()
    send_across(1, k_ref, 1)
    send_direct(1, k_ref, kbuf, 1)
    send_across(2, v_ref, 1)
    send_direct(2, v_ref, vbuf, 1)
    loads[2].wait()
    send_across(4, q_ref, -1)
    run_row = dot(rates, lower, ((1,), (1,)), exact)
    enter = [jnp.exp(at_col[h]) for h in range(heads)]
    damping = [
        jnp.where(causal, jnp.exp(jnp.where(causal, at_col[h] - run_row[h : h + 1, :], 0.0)), 0.0)
        for h in range(heads)
    ]
    for d in range(1, REACH + 1):

        @pl.when(me - d < 0)
        def _():
            kbuf[d] = jnp.zeros_like(kbuf[d])
            vbuf[d] = jnp.zeros_like(vbuf[d])
            info_left[d] = jnp.full((8, HD), -1.0, F32)

        @pl.when(me + d >= n)
        def _():
            qbuf[d] = jnp.zeros_like(qbuf[d])
            gbuf[d] = jnp.zeros_like(gbuf[d])
            sidebuf[d] = jnp.zeros((2 * heads, HD), F32)
            logsbuf[d] = jnp.zeros((2 * heads, HD), F32)
            info_right[d] = jnp.full((8, HD), -1.0, F32)

    send_small(3, info, info_right, -1)
    forward_on(1, k_ref, kbuf, 1)

    collect(0, up_send, up_recv)
    pieces = [up_recv[p] for p in range(GROUP)]
    factors = [tail_of(piece) for piece in pieces]
    terms = [piece[:HD, :].astype(F32) for piece in pieces]
    starts, state, product = scan_plane(terms, factors, range(GROUP))
    total_send[0] = with_tail(state, product)
    send_totals(0, 1)
    forward_on(2, v_ref, vbuf, 1)
    wait_totals(0, 1)
    state = incoming(0, plane)
    for p in range(GROUP):
        state_send[p] = (starts[p][1] * state + starts[p][0]).astype(BF16)
    spread(1, state_send, state_recv)

    wait_small(0, info, info_left, 1)
    wait_block(1, k_ref, kbuf, 1)
    bias = [jnp.where(causal, 0.0, NEG)]
    for d in range(1, REACH + 1):
        listed = (first == d - 1.0) | (second == d - 1.0)
        seen = (info_left[d][0:1, :] == doc) & listed
        bias.append(jnp.broadcast_to(jnp.where(seen, 0.0, NEG), (BLK, HD)))
    bias = jnp.concatenate(bias, axis=1)
    weights = []
    logsum = []
    for h in range(heads):
        keys = kbuf[:, :, cols[h]].reshape(-1, HD)
        s = nt(q_ref[:, cols[h]], keys) * scaling + bias
        score[h] = s
        m = jnp.max(s, axis=1, keepdims=True)
        e = jnp.exp(s - m)
        total = jnp.sum(e, axis=1, keepdims=True)
        weights.append((e * (1.0 / total)).astype(BF16))
        logsum.append(m + jnp.log(total))
    block = jnp.zeros((BLK, HD), F32)
    for h in range(heads):
        block = jnp.where(col_at == h, logsum[h], block)
    logs_out[...] = block.T[0 : 2 * heads, :]
    logsbuf[0] = logs_out[...]
    send_small(7, logs_out, logsbuf, -1)
    wait_block(2, v_ref, vbuf, 1)
    send_direct(4, q_ref, qbuf, -1)
    forward_on(4, q_ref, qbuf, -1)
    loads[8].wait()
    loads[9].wait()
    outs = []
    for h in range(heads):
        o = nn(weights[h], vbuf[:, :, cols[h]].reshape(-1, HD)).astype(BF16)
        outs.append(o)
        out_ref[:, cols[h]] = o
    leaves[0].start()

    mixing = [
        (nt(outs[h], lk_ref[:, cols[h]]) * damping[h]).astype(BF16) for h in range(heads)
    ]
    inner = [nn(mixing[h], lv_ref[:, cols[h]]) for h in range(heads)]
    collect(1, state_send, state_recv)
    states = state_recv[...].reshape(heads * HD, HD)
    raws = []
    scaled = []
    squares = jnp.zeros((BLK, HD), F32)
    cross = jnp.zeros((BLK, HD), F32)
    for h in range(heads):
        raw = inner[h] + enter[h] * nn(outs[h], states[h * HD : (h + 1) * HD])
        sc = cot_ref[:, cols[h]].astype(F32) * gain_ref[:, cols[h]]
        squares += raw * raw
        cross += sc * raw
        raws.append(raw)
        scaled.append(sc)
    sums[...] = jnp.where(
        col_at < HD // 2,
        jnp.sum(squares, axis=1, keepdims=True),
        jnp.sum(cross, axis=1, keepdims=True),
    )

    def to_head(o):
        return pltpu.make_async_remote_copy(
            src_ref=sums,
            dst_ref=sums_recv.at[o],
            send_sem=head_send.at[o],
            recv_sem=head_recv.at[o],
            device_id={"head": lax.rem(group + o, groups)},
            device_id_type=MESH,
        )

    for o in range(1, groups):
        to_head(o).start()
    qscaled = [(outs[h].astype(F32) * enter[h]).astype(BF16) for h in range(heads)]
    total = sums[...]
    for o in range(1, groups):
        to_head(o).wait()
        total = total + sums_recv[o]
    features = heads * HD * groups
    mean = jnp.broadcast_to(total[:, 0:1], (BLK, HD)) / features + EPSILON
    inverse = lax.rsqrt(mean)
    factor = jnp.broadcast_to(total[:, HD // 2 : HD // 2 + 1], (BLK, HD)) / (features * mean)
    halves = [((scaled[h] - raws[h] * factor) * inverse).astype(BF16) for h in range(heads)]
    mix_grads = []
    deltas = []
    gs = []
    for h in range(heads):
        mg = (nt(halves[h], lv_ref[:, cols[h]]) * damping[h]).astype(BF16)
        mix_grads.append(mg)
        g = nn(mg, lk_ref[:, cols[h]]) + enter[h] * nt(halves[h], states[h * HD : (h + 1) * HD])
        g = g.astype(BF16)
        lqg_ref[:, cols[h]] = g
        gbuf[0, :, cols[h]] = g
        gs.append(g)
    send_across(5, gbuf.at[0], -1)
    for h in range(heads):
        back = tn(qscaled[h], halves[h])
        back_send[h] = back.astype(BF16)
    spread(2, back_send, back_recv)
    send_direct(5, gbuf.at[0], gbuf, -1)
    for h in range(heads):
        g = gs[h]
        deltas.append(
            jnp.sum(g.astype(F32) * outs[h].astype(F32), axis=1, keepdims=True)
        )
    block = jnp.zeros((BLK, HD), F32)
    for h in range(heads):
        block = jnp.where(col_at == h, deltas[h], block)
    side[...] = block.T[0 : 2 * heads, :]
    sidebuf[0] = side[...]
    send_small(6, side, sidebuf, -1)
    leaves[5].start()
    for h in range(heads):
        lout_ref[:, cols[h]] = (raws[h] * inverse * gain_ref[:, cols[h]]).astype(BF16)
    leaves[4].start()
    def query_gradient(h):
        chance = jnp.exp(score[h] - logsum[h])
        cg = nt(gbuf[0, :, cols[h]], vbuf[:, :, cols[h]].reshape(-1, HD))
        sg = (chance * (cg - deltas[h])).astype(BF16)
        keys = kbuf[:, :, cols[h]].reshape(-1, HD)
        dq_ref[:, cols[h]] = (nn(sg, keys) * scaling).astype(BF16)

    for h in range(heads // 2):
        query_gradient(h)
    forward_on(5, gbuf.at[0], gbuf, -1)
    collect(2, back_send, back_recv)
    terms = [back_recv[p].astype(F32) for p in range(GROUP)]
    factors = [tail_of(up_recv[p]) for p in range(GROUP)]
    starts, state, product = scan_plane(terms, factors, range(GROUP - 1, -1, -1))
    total_send[1] = with_tail(state, product)
    send_totals(1, -1)
    for h in range(heads // 2, heads):
        query_gradient(h)
    leaves[1].start()
    key_local = [tn(mix_grads[h], outs[h]) for h in range(heads)]
    value_local = [tn(mixing[h], halves[h]) for h in range(heads)]
    wait_totals(1, -1)
    state = incoming(1, planes - 1 - plane)
    for p in range(GROUP):
        later_send[p] = (starts[p][1] * state + starts[p][0]).astype(BF16)
    spread(3, later_send, later_recv)

    wait_small(3, info, info_right, -1)
    wait_block(4, q_ref, qbuf, -1)
    bias = [jnp.where(row_at <= col_at, 0.0, NEG)]
    for d in range(1, REACH + 1):
        theirs = info_right[d]
        listed = (theirs[1:2, :] == d - 1.0) | (theirs[2:3, :] == d - 1.0)
        seen = (theirs[0:1, :] == doc) & listed
        bias.append(jnp.broadcast_to(jnp.where(seen, 0.0, NEG), (BLK, HD)))
    bias = jnp.concatenate(bias, axis=1)
    wait_small(7, logs_out, logsbuf, -1)
    for h in range(heads):
        queries = qbuf[:, :, cols[h]].reshape(-1, HD)
        logs = jnp.concatenate([logsbuf[d, h : h + 1, :] for d in range(REACH + 1)], axis=1)
        score[h] = jnp.exp(nt(k_ref[:, cols[h]], queries) * scaling + bias - logs)
    wait_block(5, gbuf.at[0], gbuf, -1)
    wait_small(6, side, sidebuf, -1)
    for h in range(heads):
        queries = qbuf[:, :, cols[h]].reshape(-1, HD)
        grads = gbuf[:, :, cols[h]].reshape(-1, HD)
        dels = jnp.concatenate(
            [sidebuf[d, h : h + 1, :] for d in range(REACH + 1)], axis=1
        )
        chance = score[h]
        dv_ref[:, cols[h]] = nn(chance.astype(BF16), grads).astype(BF16)
        cg = nt(v_ref[:, cols[h]], grads)
        sg = (chance * (cg - dels)).astype(BF16)
        dk_ref[:, cols[h]] = (nn(sg, queries) * scaling).astype(BF16)
    leaves[2].start()
    leaves[3].start()

    collect(3, later_send, later_recv)
    laters = later_recv[...].reshape(heads * HD, HD)
    for h in range(heads):
        later = laters[h * HD : (h + 1) * HD]
        lkg_ref[:, cols[h]] = (
            key_local[h] + leave[h] * nt(lv_ref[:, cols[h]], later)
        ).astype(BF16)
        lvg_ref[:, cols[h]] = (
            value_local[h] + leave[h] * nn(lk_ref[:, cols[h]], later)
        ).astype(BF16)
    leaves[6].start()
    leaves[7].start()
    wait_sent(1, k_ref, kbuf, 1)
    wait_sent(2, v_ref, vbuf, 1)
    wait_sent(4, q_ref, qbuf, -1)
    wait_sent(5, gbuf.at[0], gbuf, -1)
    for copy in leaves:
        copy.wait()


def store_all(*refs):
    held, arrived, done = refs[16:]
    loads = [pltpu.make_async_copy(refs[i], held.at[i], arrived.at[i]) for i in range(8)]
    stores = [pltpu.make_async_copy(held.at[i], refs[8 + i], done.at[i]) for i in range(8)]
    for load in loads:
        load.start()
    for load, store in zip(loads, stores):
        load.wait()
        store.start()
    for store in stores:
        store.wait()


def body(
    softmax_query,
    softmax_key,
    softmax_value,
    document_ids,
    block_lists,
    linear_key,
    linear_value,
    linear_decay,
    linear_gain,
    linear_cotangent,
):
    n = lax.axis_size("ctx")
    groups = lax.axis_size("head")
    length, width = softmax_query.shape
    heads = width // HD
    assert heads == GROUP and n % GROUP == 0
    anywhere = pl.BlockSpec(memory_space=pl.ANY)
    array = pltpu.VMEM((length, width), BF16)
    slots = REACH + 1
    window = pltpu.VMEM((slots, length, width), BF16)
    part = pltpu.VMEM((GROUP, HD, HD), BF16)
    results = pl.pallas_call(
        functools.partial(kernel, n, groups),
        out_shape=[jax.ShapeDtypeStruct((length, width), BF16)] * 8,
        in_specs=[anywhere] * 10,
        out_specs=[anywhere] * 8,
        scratch_shapes=[
            pltpu.VMEM((8, length, width), BF16),
            pltpu.SemaphoreType.DMA((8,)),
            pltpu.SMEM((1,), jnp.int32),
            pltpu.VMEM((1, 2), jnp.int32),
            array,
            array,
            pltpu.VMEM((heads, length), F32),
            pltpu.VMEM((1, width), F32),
            array,
            pltpu.SemaphoreType.DMA((10,)),
            window,
            window,
            window,
            window,
            pltpu.VMEM((8, HD), F32),
            pltpu.VMEM((slots, 8, HD), F32),
            pltpu.VMEM((slots, 8, HD), F32),
            pltpu.VMEM((2 * heads, HD), F32),
            pltpu.VMEM((slots, 2 * heads, HD), F32),
            pltpu.VMEM((2 * heads, HD), F32),
            pltpu.VMEM((slots, 2 * heads, HD), F32),
            pltpu.VMEM((heads, length, slots * HD), F32),
            pltpu.VMEM((GROUP, HD + TAIL, HD), BF16),
            pltpu.VMEM((GROUP, HD + TAIL, HD), BF16),
            part,
            part,
            part,
            part,
            part,
            part,
            pltpu.VMEM((length, HD), F32),
            pltpu.VMEM((groups, length, HD), F32),
            pltpu.VMEM((6, length, width), BF16),
            pltpu.SemaphoreType.DMA((6,)),
            pltpu.SemaphoreType.DMA((6,)),
            pltpu.SemaphoreType.DMA((8, slots)),
            pltpu.SemaphoreType.DMA((8, slots)),
            pltpu.VMEM((2, HD + TAIL, HD), BF16),
            pltpu.VMEM((2, n // GROUP, HD + TAIL, HD), BF16),
            pltpu.SemaphoreType.DMA((2, n // GROUP)),
            pltpu.SemaphoreType.DMA((2, n // GROUP)),
            pltpu.SemaphoreType.DMA((4, GROUP)),
            pltpu.SemaphoreType.DMA((4, GROUP)),
            pltpu.SemaphoreType.DMA((groups,)),
            pltpu.SemaphoreType.DMA((groups,)),
        ],
        compiler_params=pltpu.CompilerParams(
            collective_id=0, has_side_effects=True, vmem_limit_bytes=60 * 1024 * 1024
        ),
    )(
        softmax_query,
        softmax_key,
        softmax_value,
        document_ids,
        block_lists,
        linear_key,
        linear_value,
        linear_decay,
        linear_gain.reshape(1, width),
        linear_cotangent,
    )
    store = pl.pallas_call(
        store_all,
        out_shape=[jax.ShapeDtypeStruct((length, width), BF16)] * 8,
        in_specs=[anywhere] * 8,
        out_specs=[anywhere] * 8,
        scratch_shapes=[
            pltpu.VMEM((8, length, width), BF16),
            pltpu.SemaphoreType.DMA((8,)),
            pltpu.SemaphoreType.DMA((8,)),
        ],
        compiler_params=pltpu.CompilerParams(vmem_limit_bytes=60 * 1024 * 1024),
    )
    return tuple(store(*results))


def solution(mesh):
    tokens = P("ctx", "head")
    return jax.shard_map(
        body,
        mesh=mesh,
        in_specs=(
            tokens,
            tokens,
            tokens,
            P("ctx"),
            P("ctx", None),
            tokens,
            tokens,
            P("head", "ctx"),
            P("head"),
            tokens,
        ),
        out_specs=(tokens,) * 8,
        check_vma=False,
    )
```
